256 devices in a mesh: section: 2 (over z_hi), dp: 8 (over y, core), mp: 16 (over z_lo, x).
Axes of the slice: x: 4, y: 4, z: 8 (z_hi: 2, z_lo: 4; z = z_hi * 4 + z_lo), core: 2. Of those that a mesh axis runs over, the one named last changes fastest.
Arguments:
- loss_sensitivity_outgoing: bfloat16 [2, 1536, 8192], P('section', ('dp', 'mp')), may hold values from -6 to 6
- expansion_factor: bfloat16 [2, 8192, 32768], P('section', 'dp', 'mp'), may hold values from -0.0508233 to 0.0508233
- contraction_factor: bfloat16 [2, 32768, 8192], P('section', 'mp', 'dp'), may hold values from -0.03125 to 0.03125
- intermediate_affine_values: bfloat16 [2, 1536, 32768], P('section', 'dp', 'mp'), may hold values from -6 to 6
- centered_unscaled_entry: bfloat16 [2, 1536, 8192], P('section', 'mp', 'dp'), may hold values from -4.5 to 4.5
- inverse_spread_per_position: float32 [2, 1536], P('section', 'mp'), may hold values from 0.3 to 3
- layernorm_multiplier: float32 [2, 8192], P('section', 'dp'), may hold values from 0.25 to 3
Outputs:
- grad_out: bfloat16 [2, 1536, 8192], P('section', 'mp', 'dp')
The draws below stay inside these ranges and needn't reach their ends.
All inputs are finite; a program needn't handle non-finite values.
Results may differ from the reference program's by a relative error of at most 0.02.
Values may be sent and summed in bfloat16 or wider, within the bound.
No kernel may reach another device: no remote copies, remote signals or barrier semaphores. Data moves between devices by JAX's collectives and lax.ppermute only.
A program may use at most 64 MiB of HBM per device.

```python
import math
import jax
import jax.numpy as jnp
from jax import lax

D = 8192
FF = 32768
ROWS = 1536
N_SECTION = 2
N_DP = 8
N_MP = 16


def draw_expansion_factor(key, part):
    key = jax.random.fold_in(key, 11)
    noise_key, unit_key = jax.random.split(key)
    noise = jnp.clip(jax.random.normal(noise_key, (N_SECTION, D, FF), jnp.float32), -3.0, 3.0)
    shared = jnp.clip(jax.random.normal(unit_key, (N_SECTION, 1, FF), jnp.float32), -2.0, 2.0)
    return ((noise + 0.8 * shared) * D ** (-0.5)).astype(jnp.bfloat16)


def draw_centered_unscaled_entry(key, part):
    key = jax.random.fold_in(key, 12)
    noise_key, row_key = jax.random.split(key)
    noise = jnp.clip(jax.random.normal(noise_key, (N_SECTION, ROWS, D), jnp.float32), -3.0, 3.0)
    offset = jax.random.uniform(row_key, (N_SECTION, ROWS, 1), jnp.float32, -1.5, 1.5)
    return (noise + offset).astype(jnp.bfloat16)


def draw_layernorm_multiplier(key, part):
    key = jax.random.fold_in(key, 13)
    base_key = jax.random.fold_in(key, 0)
    base = jax.random.uniform(base_key, (N_SECTION, D), jnp.float32, 0.5, 1.5)
    return base.astype(jnp.float32)


def levels(own_key, dims, cuts, least, high):
    def one(axis_at, blocks):
        heights = jax.random.uniform(jax.random.fold_in(jax.random.fold_in(own_key, 6), axis_at), (blocks,), jnp.float32, least / len(cuts), high / len(cuts))
        return jnp.repeat(jnp.exp(heights), dims[axis_at] // blocks).reshape((-1,) + (1,) * (len(dims) - axis_at - 1))

    level = one(*cuts[0])
    for cut in cuts[1:]:
        level = level * one(*cut)
    return level


def normal_values(stream_key, extent, scale, most, shards=(), kind=jnp.bfloat16):
    factor_of = levels(stream_key, extent, shards, -0.22, 0.18) if shards else 1.0
    drawn = jax.random.normal(stream_key, extent, jnp.float32) * scale * factor_of
    return jnp.minimum(jnp.maximum(drawn, -most), most).astype(kind)


def setup_inputs(seed: int = 0) -> dict:
    key_list = jax.random.split(jax.random.key(seed), 8)
    loss_sensitivity_outgoing = normal_values(key_list[0], (N_SECTION, ROWS, D), 1.0, 6.0, ((0, 2), (1, 128)))
    expansion_factor = draw_expansion_factor(jax.random.fold_in(key_list[7], 71), 0)
    contraction_factor = normal_values(key_list[2], (N_SECTION, FF, D), FF ** -0.5, 0.03125, ((0, 2), (1, 16), (2, 8)))
    intermediate_affine_values = normal_values(key_list[3], (N_SECTION, ROWS, FF), 1.5, 6.0, ((0, 2), (1, 8), (2, 16)))
    centered_unscaled_entry = draw_centered_unscaled_entry(jax.random.fold_in(key_list[7], 71), 0)
    inverse_spread_per_position = jnp.clip(jnp.exp(math.log(3.0) - 2.3025851 * jax.random.uniform(key_list[5], (N_SECTION, ROWS), jnp.float32) ** levels(key_list[5], (N_SECTION, ROWS), ((0, 2), (1, 16)), -0.2, 0.2)), 0.3, 3.0)
    layernorm_multiplier = draw_layernorm_multiplier(jax.random.fold_in(key_list[7], 71), 0)
    return {"loss_sensitivity_outgoing": loss_sensitivity_outgoing, "expansion_factor": expansion_factor, "contraction_factor": contraction_factor, "intermediate_affine_values": intermediate_affine_values, "centered_unscaled_entry": centered_unscaled_entry, "inverse_spread_per_position": inverse_spread_per_position, "layernorm_multiplier": layernorm_multiplier}


def gelu_slope(u):
    c = math.sqrt(2.0 / math.pi)
    t = jnp.tanh(c * (u + 0.044715 * u * u * u))
    return 0.5 * (1.0 + t) + 0.5 * u * (1.0 - t * t) * c * (1.0 + 3.0 * 0.044715 * u * u)

def blocked_product(left, right_t, blocks):
    width = left.shape[1] // blocks
    total = jnp.zeros((left.shape[0], right_t.shape[0]), jnp.float32)
    for index in range(blocks):
        piece = jnp.dot(left[:, index * width:(index + 1) * width], right_t[:, index * width:(index + 1) * width].T, preferred_element_type=jnp.float32)
        total = total + piece.astype(jnp.bfloat16).astype(jnp.float32)
    return total

def reference(loss_sensitivity_outgoing, expansion_factor, contraction_factor, intermediate_affine_values, centered_unscaled_entry, inverse_spread_per_position, layernorm_multiplier):
    results = []
    for cohort_identifier in range(N_SECTION):
        upstream = loss_sensitivity_outgoing[N_SECTION - 1 - cohort_identifier]
        grad_hidden = blocked_product(upstream, contraction_factor[cohort_identifier], N_DP)
        slope = (grad_hidden * gelu_slope(intermediate_affine_values[cohort_identifier].astype(jnp.float32))).astype(jnp.bfloat16)
        grad_norm = blocked_product(slope, expansion_factor[cohort_identifier], N_MP)
        scaled = layernorm_multiplier[cohort_identifier][None, :] * grad_norm
        standardized_entry = centered_unscaled_entry[cohort_identifier].astype(jnp.float32)
        first = lax.optimization_barrier(jnp.sum(scaled, axis=1))
        second = lax.optimization_barrier(jnp.sum(scaled * standardized_entry, axis=1))
        result = upstream.astype(jnp.float32) + inverse_spread_per_position[cohort_identifier][:, None] * (scaled - first[:, None] / D - standardized_entry * second[:, None] / D)
        results.append(result.astype(jnp.bfloat16))
    return jnp.stack(results)
```

```python
import functools
import math

import jax
import jax.numpy as jnp
from jax import lax
from jax.experimental import pallas as pl
from jax.experimental.pallas import tpu as pltpu
from jax.sharding import Mesh, PartitionSpec as P

BF = jnp.bfloat16
F32 = jnp.float32
CHUNKS = 3


def move_z(array, flip):
    return lax.ppermute(array, "z", [(z, z ^ flip) for z in range(4)])


def move_section(array, flip):
    pairs = [(4 * s + z, 4 * (1 - s) + (z ^ flip)) for s in range(2) for z in range(4)]
    return lax.ppermute(array, ("section", "z"), pairs)


def move_core(array):
    return lax.ppermute(array, "core", [(0, 1), (1, 0)])


def gelu_slope(u):
    c = math.sqrt(2.0 / math.pi)
    t = jnp.tanh(c * (u + 0.044715 * u * u * u))
    return 0.5 * (1.0 + t) + 0.5 * u * (1.0 - t * t) * c * (1.0 + 3.0 * 0.044715 * u * u)


def nt_dot(left, right):
    return lax.dot_general(left, right, (((1,), (1,)), ((), ())), preferred_element_type=F32)


def full(shape):
    return pl.BlockSpec(shape, lambda i: (0,) * len(shape))


def hidden_kernel(pos, gathered, weight, send, keep, mine, lhs):
    x, y, z, c = pos[0], pos[1], pos[2], pos[3]

    @pl.when(pl.program_id(0) == 0)
    def _():
        for c_rel in range(2):
            for y_at in range(4):
                source = 2 * y_at + jnp.bitwise_xor(c, c_rel)
                for x_at in range(4):
                    lhs[4 * c_rel + y_at, x_at] = gathered[x_at, source]
        rows = lhs[4 * jnp.bitwise_xor(c, x // 2) + z].astype(F32).reshape(4, 2, 8, -1)
        picked = jnp.where(lax.rem(x, 2) == 0, rows[:, 0], rows[:, 1])
        mine[...] = picked.reshape(32, -1).astype(BF)

    rows = lhs[...].reshape(512, -1)
    product = nt_dot(rows, weight[...]).astype(BF)
    keep[...] = product[:256].reshape(keep.shape)
    send[...] = product[256:].reshape(send.shape)


def hidden_product(pos, gathered, weight):
    width = weight.shape[0]
    depth = weight.shape[1]
    tile = min(512, width)
    out_block = pl.BlockSpec((4, 64, tile), lambda i: (0, 0, i))
    return pl.pallas_call(
        hidden_kernel,
        grid=(width // tile,),
        in_specs=[
            pl.BlockSpec(memory_space=pltpu.SMEM),
            full(gathered.shape),
            pl.BlockSpec((tile, depth), lambda i: (i, 0)),
        ],
        out_specs=[out_block, out_block, full((32, depth))],
        out_shape=[
            jax.ShapeDtypeStruct((4, 64, width), BF),
            jax.ShapeDtypeStruct((4, 64, width), BF),
            jax.ShapeDtypeStruct((32, depth), BF),
        ],
        scratch_shapes=[pltpu.VMEM((8, 4, 16, depth), BF)],
        compiler_params=pltpu.CompilerParams(vmem_limit_bytes=40 * 2**20),
        cost_estimate=pl.CostEstimate(
            flops=2 * 512 * width * depth, bytes_accessed=2 * (width * depth + 512 * (width + depth)), transcendentals=0
        ),
    )(pos, gathered, weight)


def feature_kernel(pos, same, other, weight, out, lhs, result):
    c = pos[3]

    @pl.when(pl.program_id(0) == 0)
    def _():
        for y_at in range(4):
            lhs[2 * y_at + c] = same[y_at]
            lhs[2 * y_at + 1 - c] = other[y_at]

    rows = lhs[...].reshape(512, -1)
    result[...] = nt_dot(rows, weight[...]).reshape(result.shape)
    for x_at in range(4):
        for z_at in range(4):
            rows = result[2 * z_at + x_at // 2, :, x_at % 2]
            out[x_at, z_at] = rows.reshape(32, -1).astype(BF)


def feature_product(pos, same, other, weight):
    width = weight.shape[0]
    depth = weight.shape[1]
    tile = min(256, width)
    return pl.pallas_call(
        feature_kernel,
        grid=(width // tile,),
        in_specs=[
            pl.BlockSpec(memory_space=pltpu.SMEM),
            full(same.shape),
            full(other.shape),
            pl.BlockSpec((tile, depth), lambda i: (i, 0)),
        ],
        out_specs=pl.BlockSpec((4, 4, 32, tile), lambda i: (0, 0, 0, i)),
        out_shape=jax.ShapeDtypeStruct((4, 4, 32, width), BF),
        scratch_shapes=[pltpu.VMEM((8, 64, depth), BF), pltpu.VMEM((8, 4, 2, 8, tile), F32)],
        compiler_params=pltpu.CompilerParams(vmem_limit_bytes=40 * 2**20),
        cost_estimate=pl.CostEstimate(
            flops=2 * 512 * width * depth, bytes_accessed=2 * (width * depth + 512 * (width + depth)), transcendentals=0
        ),
    )(pos, same, other, weight)


def add(*terms):
    return functools.reduce(jnp.add, [term.astype(F32) for term in terms])


def gather_rows(part, z):
    arrived = [move_section(part, flip) for flip in range(4)]
    odd, high = z % 2 == 1, z >= 2
    a0, a1, a2, a3 = arrived
    a0, a1 = jnp.where(odd, a1, a0), jnp.where(odd, a0, a1)
    a2, a3 = jnp.where(odd, a3, a2), jnp.where(odd, a2, a3)
    a0, a2 = jnp.where(high, a2, a0), jnp.where(high, a0, a2)
    a1, a3 = jnp.where(high, a3, a1), jnp.where(high, a1, a3)
    depth = part.shape[-1]
    own = jnp.stack([a0, a1, a2, a3]).reshape(2, 2, 4, 8, depth).transpose(3, 0, 2, 1, 4).reshape(8, 16, depth)
    return lax.all_gather(own, "x", axis=0)


def reduce_hidden(send, keep):
    total = add(keep, move_core(send)).astype(BF)
    return lax.psum_scatter(total, "y", scatter_dimension=0).astype(F32)


def reduce_features(parts, z):
    total = lax.psum_scatter(parts, "x", scatter_dimension=0)

    def block(index):
        return lax.dynamic_index_in_dim(total, index, 0, keepdims=False)

    terms = [move_z(block(z ^ flip), flip) for flip in (1, 2, 3)]
    return add(block(z), *terms)


def per_device(
    loss_sensitivity_outgoing,
    expansion_factor,
    contraction_factor,
    intermediate_affine_values,
    centered_unscaled_entry,
    inverse_spread_per_position,
    layernorm_multiplier,
):
    x, y, z, c = (lax.axis_index(name) for name in ("x", "y", "z", "core"))
    pos = jnp.stack([x, y, z, c]).astype(jnp.int32)
    model = 8 * expansion_factor.shape[1]
    rows = lax.all_to_all(loss_sensitivity_outgoing[0], ("y", "core"), split_axis=1, concat_axis=0, tiled=True)
    rows = rows.reshape(8, 12, -1).transpose(1, 0, 2)

    hidden = intermediate_affine_values.shape[-1]
    slope = intermediate_affine_values[0].reshape(2, 2, 4, CHUNKS, 4, hidden)
    slope = gelu_slope(slope.transpose(3, 2, 0, 4, 1, 5).reshape(CHUNKS, 64, hidden).astype(F32))

    def by_chunk(array):
        rest = array.shape[1:]
        array = array.reshape(2, 4, CHUNKS, 4, *rest)
        array = array.transpose(2, 1, 3, 0, *range(4, array.ndim))
        return array.reshape(CHUNKS, 32, *rest)

    entry = by_chunk(centered_unscaled_entry[0]).astype(F32)
    spread = by_chunk(inverse_spread_per_position[0])
    gain = layernorm_multiplier[0]

    mine, scaled = [], []
    for k in range(CHUNKS):
        gathered = gather_rows(rows[4 * k : 4 * k + 4], z)
        send, keep, own_rows = hidden_product(pos, gathered, contraction_factor[0])
        block = (reduce_hidden(send, keep) * slope[k]).astype(BF)
        same = lax.all_gather(block, "y", axis=0)
        parts = feature_product(pos, same, move_core(same), expansion_factor[0])
        mine.append(own_rows)
        scaled.append(gain * reduce_features(parts, z))
    scaled = jnp.stack(scaled)
    upstream = jnp.stack(mine).astype(F32)
    sums = lax.psum(jnp.stack([jnp.sum(scaled, axis=2), jnp.sum(scaled * entry, axis=2)]), ("y", "core"))
    result = upstream + spread[:, :, None] * (
        scaled - sums[0][:, :, None] / model - entry * sums[1][:, :, None] / model
    )
    result = result.reshape(CHUNKS, 4, 4, 2, -1).transpose(3, 1, 0, 2, 4)
    return result.reshape(1, 96, -1).astype(BF)


def solution(mesh):
    split = Mesh(mesh.devices.reshape(2, 4, 2, 4, 4), ("section", "y", "core", "z", "x"))
    dp, mp = ("y", "core"), ("z", "x")
    in_specs = (
        P("section", dp + mp, None),
        P("section", dp, mp),
        P("section", mp, dp),
        P("section", dp, mp),
        P("section", mp, dp),
        P("section", mp),
        P("section", dp),
    )
    out_specs = P("section", mp, dp)
    return jax.shard_map(per_device, mesh=split, in_specs=in_specs, out_specs=out_specs, check_vma=False)
```

```python
import functools
import math

import jax
import jax.numpy as jnp
from jax import lax
from jax.experimental import pallas as pl
from jax.experimental.pallas import tpu as pltpu
from jax.sharding import Mesh, PartitionSpec as P

BF = jnp.bfloat16
F32 = jnp.float32
CHUNKS = 3
ROWS = 12 // CHUNKS


def near(core):
    return 1 + 2 * core


def wide(core):
    return 3 - 2 * core


def move_ring(array, axis, flip):
    pairs = [(c, i, c, i ^ flip(c)) for c in range(2) for i in range(4)]
    if axis == "y":
        return lax.ppermute(array, ("y", "core"), [(2 * i + c, 2 * j + d) for c, i, d, j in pairs])
    return lax.ppermute(array, ("core", axis), [(4 * c + i, 4 * d + j) for c, i, d, j in pairs])


def move_z(array, flip):
    return lax.ppermute(array, "z", [(z, z ^ flip) for z in range(4)])


def move_mirror(array):
    return lax.ppermute(array, ("section", "z"), [(i, 7 - i) for i in range(8)])


def move_core(array):
    return lax.ppermute(array, "core", [(0, 1), (1, 0)])


def ring_order(core):
    return 0, near(core), wide(core), 2


def gelu_slope(u):
    c = math.sqrt(2.0 / math.pi)
    t = jnp.tanh(c * (u + 0.044715 * u * u * u))
    return 0.5 * (1.0 + t) + 0.5 * u * (1.0 - t * t) * c * (1.0 + 3.0 * 0.044715 * u * u)


def nt_dot(left, right):
    return lax.dot_general(left, right, (((1,), (1,)), ((), ())), preferred_element_type=F32)


def full(shape):
    return pl.BlockSpec(shape, lambda i: (0,) * len(shape))


SMEM = pl.BlockSpec(memory_space=pltpu.SMEM)


def slope_kernel(u, *outs):
    values = gelu_slope(u[...].astype(F32))
    for k in range(CHUNKS):
        pieces = []
        for x in range(4):
            for z in range(4):
                start = (4 * z + x) * 12 + ROWS * k
                pieces.append(values[start : start + ROWS])
        outs[k][...] = jnp.concatenate(pieces, axis=0)


def slope_rows(u):
    rows, width = u.shape
    tile = min(512, width)
    return pl.pallas_call(
        slope_kernel,
        grid=(width // tile,),
        in_specs=[pl.BlockSpec((rows, tile), lambda i: (0, i))],
        out_specs=[pl.BlockSpec((rows // CHUNKS, tile), lambda i: (0, i))] * CHUNKS,
        out_shape=[jax.ShapeDtypeStruct((rows // CHUNKS, width), F32)] * CHUNKS,
        compiler_params=pltpu.CompilerParams(vmem_limit_bytes=16 * 2**20),
        cost_estimate=pl.CostEstimate(flops=20 * rows * width, bytes_accessed=6 * rows * width, transcendentals=rows * width),
    )(u)


def hidden_kernel(pos, near_pair, wide_pair, weight, keep, send, mine, lhs):
    x, y, z, c = pos[0], pos[1], pos[2], pos[3]

    @pl.when(pl.program_id(0) == 0)
    def _():
        for c_rel in range(2):
            core = jnp.bitwise_xor(c, c_rel)
            for j, flip in enumerate(ring_order(core)):
                source = 2 * jnp.bitwise_xor(y, flip) + core
                for x_rel, x_flip in enumerate(ring_order(c)):
                    ref = near_pair if x_rel < 2 else wide_pair
                    lhs[4 * c_rel + j, jnp.bitwise_xor(x, x_flip)] = ref[x_rel % 2, source]
        source = 2 * z + x // 2
        for x_rel, x_flip in enumerate(ring_order(c)):
            ref = near_pair if x_rel < 2 else wide_pair
            rows = ref[x_rel % 2, source].astype(F32)
            picked = jnp.where(lax.rem(x, 2) == 0, rows[:8], rows[8:])
            mine[jnp.bitwise_xor(x, x_flip)] = picked

    rows = lhs[...].reshape(512, -1)
    product = nt_dot(rows, weight[...]).astype(BF)
    keep[...] = product[:256].reshape(keep.shape)
    send[...] = product[256:].reshape(send.shape)


def hidden_product(pos, near_pair, wide_pair, weight):
    width, depth = weight.shape
    tile = min(512, width)
    out_block = pl.BlockSpec((4, 64, tile), lambda i: (0, 0, i))
    return pl.pallas_call(
        hidden_kernel,
        grid=(width // tile,),
        in_specs=[
            SMEM,
            full(near_pair.shape),
            full(wide_pair.shape),
            pl.BlockSpec((tile, depth), lambda i: (i, 0)),
        ],
        out_specs=[out_block, out_block, full((4, 8, depth))],
        out_shape=[
            jax.ShapeDtypeStruct((4, 64, width), BF),
            jax.ShapeDtypeStruct((4, 64, width), BF),
            jax.ShapeDtypeStruct((4, 8, depth), F32),
        ],
        scratch_shapes=[pltpu.VMEM((8, 4, 16, depth), BF)],
        compiler_params=pltpu.CompilerParams(vmem_limit_bytes=16 * 2**20),
        cost_estimate=pl.CostEstimate(
            flops=2 * 512 * width * depth, bytes_accessed=2 * (width * depth + 512 * (width + depth)), transcendentals=0
        ),
    )(pos, near_pair, wide_pair, weight)


def feature_kernel(pos, near_same, wide_same, near_other, wide_other, weight, keep, send, lhs, result):
    x, y, z, c = pos[0], pos[1], pos[2], pos[3]

    @pl.when(pl.program_id(0) == 0)
    def _():
        for c_rel, (near_pair, wide_pair) in enumerate(((near_same, wide_same), (near_other, wide_other))):
            core = jnp.bitwise_xor(c, c_rel)
            for j, flip in enumerate(ring_order(core)):
                ref = near_pair if j < 2 else wide_pair
                lhs[2 * jnp.bitwise_xor(y, flip) + core] = ref[j % 2]

    rows = lhs[...].reshape(512, -1)
    result[...] = nt_dot(rows, weight[...]).reshape(result.shape)
    for x_rel, x_flip in enumerate(ring_order(c)):
        to = jnp.bitwise_xor(x, x_flip)
        out = keep if x_rel < 2 else send
        for z_rel, z_flip in enumerate((0, 2, 1, 3)):
            rows = result[2 * jnp.bitwise_xor(z, z_flip) + to // 2, :, lax.rem(to, 2)]
            out[x_rel % 2, z_rel] = rows.reshape(32, -1).astype(BF)


def feature_product(pos, pairs, weight):
    width, depth = weight.shape
    tile = min(256, width)
    out_block = pl.BlockSpec((2, 4, 32, tile), lambda i: (0, 0, 0, i))
    return pl.pallas_call(
        feature_kernel,
        grid=(width // tile,),
        in_specs=[SMEM] + [full(pair.shape) for pair in pairs] + [pl.BlockSpec((tile, depth), lambda i: (i, 0))],
        out_specs=[out_block, out_block],
        out_shape=[jax.ShapeDtypeStruct((2, 4, 32, width), BF)] * 2,
        scratch_shapes=[pltpu.VMEM((8, 64, depth), BF), pltpu.VMEM((8, 4, 2, 8, tile), F32)],
        compiler_params=pltpu.CompilerParams(vmem_limit_bytes=20 * 2**20),
        cost_estimate=pl.CostEstimate(
            flops=2 * 512 * width * depth, bytes_accessed=2 * (width * depth + 512 * (width + depth)), transcendentals=0
        ),
    )(pos, *pairs, weight)


def add(*terms):
    return functools.reduce(jnp.add, [term.astype(F32) for term in terms])


def gather_rows(part, z):
    a3 = move_mirror(part)
    a1 = move_z(a3, 2)
    a2, a0 = move_z(jnp.stack([a3, a1]), 1)
    odd, high = z % 2 == 1, z >= 2
    a0, a1 = jnp.where(odd, a1, a0), jnp.where(odd, a0, a1)
    a2, a3 = jnp.where(odd, a3, a2), jnp.where(odd, a2, a3)
    a0, a2 = jnp.where(high, a2, a0), jnp.where(high, a0, a2)
    a1, a3 = jnp.where(high, a3, a1), jnp.where(high, a1, a3)
    own = jnp.concatenate([a0, a1, a2, a3]).transpose(1, 0, 2)
    return gather_ring(own, "x")


def gather_ring(block, axis):
    pair = jnp.stack([block, move_ring(block, axis, near)])
    return pair, move_ring(pair, axis, wide)


def reduce_ring(keep, send, axis):
    first = move_ring(send, axis, wide)
    second = move_ring(add(keep[1], first[1]).astype(BF), axis, near)
    return add(keep[0], first[0], second)


def reduce_hidden(keep, send):
    other = move_core(send)
    first = move_ring(add(keep[2:], other[2:]).astype(BF), "y", wide)
    second = move_ring(add(keep[1], other[1], first[1]).astype(BF), "y", near)
    return add(keep[0], other[0], first[0], second)


def reduce_features(keep, send):
    total = reduce_ring(keep, send, "x")
    first = move_z(total[2:].astype(BF), 1)
    second = move_z(add(total[1], first[1]).astype(BF), 2)
    return add(total[0], first[0], second)


def sum_over_dp(array):
    array = array + move_core(array)
    array = array + move_ring(array, "y", near)
    return array + move_ring(array, "y", wide)


def per_device(
    loss_sensitivity_outgoing,
    expansion_factor,
    contraction_factor,
    intermediate_affine_values,
    centered_unscaled_entry,
    inverse_spread_per_position,
    layernorm_multiplier,
):
    x, y, z, c = (lax.axis_index(name) for name in ("x", "y", "z", "core"))
    pos = jnp.stack([x, y, z, c]).astype(jnp.int32)
    model = 8 * expansion_factor.shape[1]
    rows = lax.all_to_all(loss_sensitivity_outgoing[0], ("y", "core"), split_axis=1, concat_axis=0, tiled=True)
    rows = rows.reshape(8, 12, -1).transpose(1, 0, 2)
    slope = slope_rows(intermediate_affine_values[0])

    def by_chunk(array):
        rest = array.shape[1:]
        array = array.reshape(2, 4, CHUNKS, ROWS, *rest)
        array = array.transpose(2, 1, 0, 3, *range(4, array.ndim))
        return array.reshape(CHUNKS, 32, *rest)

    entry = by_chunk(centered_unscaled_entry[0]).astype(F32)
    spread = by_chunk(inverse_spread_per_position[0])
    gain = layernorm_multiplier[0]

    mine, scaled = [], []
    for k in range(CHUNKS):
        gathered = gather_rows(rows[ROWS * k : ROWS * (k + 1)], z)
        keep, send, own_rows = hidden_product(pos, *gathered, contraction_factor[0])
        block = (reduce_hidden(keep, send) * slope[k]).astype(BF)
        near_pair, wide_pair = gather_ring(block, "y")
        pairs = (near_pair, wide_pair, move_core(near_pair), move_core(wide_pair))
        keep, send = feature_product(pos, pairs, expansion_factor[0])
        mine.append(own_rows.reshape(32, -1))
        scaled.append(gain * reduce_features(keep, send))
    scaled = jnp.stack(scaled)
    upstream = jnp.stack(mine)
    sums = sum_over_dp(jnp.stack([jnp.sum(scaled, axis=2), jnp.sum(scaled * entry, axis=2)]))
    result = upstream + spread[:, :, None] * (
        scaled - sums[0][:, :, None] / model - entry * sums[1][:, :, None] / model
    )
    result = result.reshape(CHUNKS, 4, 2, ROWS, -1).transpose(2, 1, 0, 3, 4)
    return result.reshape(1, 96, -1).astype(BF)


def solution(mesh):
    split = Mesh(mesh.devices.reshape(2, 4, 2, 4, 4), ("section", "y", "core", "z", "x"))
    dp, mp = ("y", "core"), ("z", "x")
    in_specs = (
        P("section", dp + mp, None),
        P("section", dp, mp),
        P("section", mp, dp),
        P("section", dp, mp),
        P("section", mp, dp),
        P("section", mp),
        P("section", dp),
    )
    out_specs = P("section", mp, dp)
    return jax.shard_map(per_device, mesh=split, in_specs=in_specs, out_specs=out_specs, check_vma=False)
```

```python
import functools
import math

import jax
import jax.numpy as jnp
from jax import lax
from jax.experimental import pallas as pl
from jax.experimental.pallas import tpu as pltpu
from jax.sharding import Mesh, PartitionSpec as P

BF = jnp.bfloat16
F32 = jnp.float32
CHUNKS = 3
ROWS = 12 // CHUNKS


def near(core):
    return 1 + 2 * core


def wide(core):
    return 3 - 2 * core


def move_ring(array, axis, flip):
    pairs = [(c, i, c, i ^ flip(c)) for c in range(2) for i in range(4)]
    if axis == "y":
        return lax.ppermute(array, ("y", "core"), [(2 * i + c, 2 * j + d) for c, i, d, j in pairs])
    return lax.ppermute(array, ("core", axis), [(4 * c + i, 4 * d + j) for c, i, d, j in pairs])


def move_y(array, flip):
    return lax.ppermute(array, "y", [(y, y ^ flip) for y in range(4)])


def move_z(array, flip):
    return lax.ppermute(array, "z", [(z, z ^ flip) for z in range(4)])


def move_mirror(array):
    return lax.ppermute(array, ("section", "z"), [(i, 7 - i) for i in range(8)])


def move_core(array):
    return lax.ppermute(array, "core", [(0, 1), (1, 0)])


def flips(chunk):
    return (near, wide) if chunk % 2 == 0 else (wide, near)


def ring_order(chunk, core):
    first, second = flips(chunk)
    return 0, first(core), second(core), 2


def gelu_slope(u):
    c = math.sqrt(2.0 / math.pi)
    t = jnp.tanh(c * (u + 0.044715 * u * u * u))
    return 0.5 * (1.0 + t) + 0.5 * u * (1.0 - t * t) * c * (1.0 + 3.0 * 0.044715 * u * u)


def nt_dot(left, right):
    return lax.dot_general(left, right, (((1,), (1,)), ((), ())), preferred_element_type=F32)


def full(shape):
    return pl.BlockSpec(shape, lambda i: (0,) * len(shape))


SMEM = pl.BlockSpec(memory_space=pltpu.SMEM)


def slope_kernel(u, *outs):
    values = gelu_slope(u[...].astype(F32))
    for k in range(CHUNKS):
        pieces = []
        for x in range(4):
            for z in range(4):
                start = (4 * z + x) * 12 + ROWS * k
                pieces.append(values[start : start + ROWS])
        outs[k][...] = jnp.concatenate(pieces, axis=0)


def slope_rows(u):
    rows, width = u.shape
    tile = min(512, width)
    return pl.pallas_call(
        slope_kernel,
        grid=(width // tile,),
        in_specs=[pl.BlockSpec((rows, tile), lambda i: (0, i))],
        out_specs=[pl.BlockSpec((rows // CHUNKS, tile), lambda i: (0, i))] * CHUNKS,
        out_shape=[jax.ShapeDtypeStruct((rows // CHUNKS, width), F32)] * CHUNKS,
        compiler_params=pltpu.CompilerParams(vmem_limit_bytes=16 * 2**20),
        cost_estimate=pl.CostEstimate(flops=20 * rows * width, bytes_accessed=6 * rows * width, transcendentals=rows * width),
    )(u)


def hidden_kernel(chunk, pos, near_pair, wide_pair, weight, keep, send, mine, lhs):
    x, y, z, c = pos[0], pos[1], pos[2], pos[3]

    @pl.when(pl.program_id(0) == 0)
    def _():
        for c_rel in range(2):
            core = jnp.bitwise_xor(c, c_rel)
            for j, flip in enumerate(ring_order(chunk, core)):
                source = 2 * jnp.bitwise_xor(y, flip) + core
                for x_rel, x_flip in enumerate(ring_order(chunk, c)):
                    ref = near_pair if x_rel < 2 else wide_pair
                    lhs[4 * c_rel + j, jnp.bitwise_xor(x, x_flip)] = ref[x_rel % 2, source]
        source = 2 * z + x // 2
        for x_rel, x_flip in enumerate(ring_order(chunk, c)):
            ref = near_pair if x_rel < 2 else wide_pair
            rows = ref[x_rel % 2, source].astype(F32)
            picked = jnp.where(lax.rem(x, 2) == 0, rows[:8], rows[8:])
            mine[jnp.bitwise_xor(x, x_flip)] = picked

    rows = lhs[...].reshape(512, -1)
    product = nt_dot(rows, weight[...]).astype(BF)
    keep[...] = product[:256].reshape(keep.shape)
    send[...] = product[256:].reshape(send.shape)


def hidden_product(chunk, pos, near_pair, wide_pair, weight):
    width, depth = weight.shape
    tile = min(512, width)
    out_block = pl.BlockSpec((4, 64, tile), lambda i: (0, 0, i))
    return pl.pallas_call(
        functools.partial(hidden_kernel, chunk),
        grid=(width // tile,),
        in_specs=[
            SMEM,
            full(near_pair.shape),
            full(wide_pair.shape),
            pl.BlockSpec((tile, depth), lambda i: (i, 0)),
        ],
        out_specs=[out_block, out_block, full((4, 8, depth))],
        out_shape=[
            jax.ShapeDtypeStruct((4, 64, width), BF),
            jax.ShapeDtypeStruct((4, 64, width), BF),
            jax.ShapeDtypeStruct((4, 8, depth), F32),
        ],
        scratch_shapes=[pltpu.VMEM((8, 4, 16, depth), BF)],
        compiler_params=pltpu.CompilerParams(vmem_limit_bytes=16 * 2**20),
        cost_estimate=pl.CostEstimate(
            flops=2 * 512 * width * depth, bytes_accessed=2 * (width * depth + 512 * (width + depth)), transcendentals=0
        ),
    )(pos, near_pair, wide_pair, weight)


def feature_kernel(chunk, pos, near_same, wide_same, near_other, wide_other, weight, keep, send, lhs, result):
    x, y, z, c = pos[0], pos[1], pos[2], pos[3]

    @pl.when(pl.program_id(0) == 0)
    def _():
        for c_rel, (near_pair, wide_pair) in enumerate(((near_same, wide_same), (near_other, wide_other))):
            core = jnp.bitwise_xor(c, c_rel)
            for j, flip in enumerate(ring_order(chunk, core)):
                ref = near_pair if j < 2 else wide_pair
                lhs[2 * jnp.bitwise_xor(y, flip) + core] = ref[j % 2]

    rows = lhs[...].reshape(512, -1)
    result[...] = nt_dot(rows, weight[...]).reshape(result.shape)
    for x_rel, x_flip in enumerate(ring_order(chunk, c)):
        to = jnp.bitwise_xor(x, x_flip)
        out = keep if x_rel < 2 else send
        for z_rel, z_flip in enumerate((0, 2, 1, 3)):
            rows = result[2 * jnp.bitwise_xor(z, z_flip) + to // 2, :, lax.rem(to, 2)]
            out[x_rel % 2, z_rel] = rows.reshape(32, -1).astype(BF)


def feature_product(chunk, pos, pairs, weight):
    width, depth = weight.shape
    tile = min(256, width)
    out_block = pl.BlockSpec((2, 4, 32, tile), lambda i: (0, 0, 0, i))
    return pl.pallas_call(
        functools.partial(feature_kernel, chunk),
        grid=(width // tile,),
        in_specs=[SMEM] + [full(pair.shape) for pair in pairs] + [pl.BlockSpec((tile, depth), lambda i: (i, 0))],
        out_specs=[out_block, out_block],
        out_shape=[jax.ShapeDtypeStruct((2, 4, 32, width), BF)] * 2,
        scratch_shapes=[pltpu.VMEM((8, 64, depth), BF), pltpu.VMEM((8, 4, 2, 8, tile), F32)],
        compiler_params=pltpu.CompilerParams(vmem_limit_bytes=20 * 2**20),
        cost_estimate=pl.CostEstimate(
            flops=2 * 512 * width * depth, bytes_accessed=2 * (width * depth + 512 * (width + depth)), transcendentals=0
        ),
    )(pos, *pairs, weight)


def add(*terms):
    return functools.reduce(jnp.add, [term.astype(F32) for term in terms])


def sort_flips(pieces, at):
    a0, a1, a2, a3 = pieces
    odd, high = at % 2 == 1, at >= 2
    a0, a1 = jnp.where(odd, a1, a0), jnp.where(odd, a0, a1)
    a2, a3 = jnp.where(odd, a3, a2), jnp.where(odd, a2, a3)
    a0, a2 = jnp.where(high, a2, a0), jnp.where(high, a0, a2)
    a1, a3 = jnp.where(high, a3, a1), jnp.where(high, a1, a3)
    return a0, a1, a2, a3


def own_features(rows, y, c):
    depth = rows.shape[1] // 8
    parts = [jnp.stack([rows[:, (2 * i + core) * depth :][:, :depth] for i in range(4)]) for core in range(2)]
    low = c == 0
    mine = jnp.where(low, parts[0], parts[1])
    other = move_core(jnp.where(low, parts[1], parts[0]))
    both = jnp.stack([jnp.where(low, mine, other), jnp.where(low, other, mine)], axis=1)

    def block(flip):
        return lax.dynamic_index_in_dim(both, y ^ flip, 0, keepdims=False)

    pieces = [block(0)] + [move_y(block(flip), flip) for flip in (1, 2, 3)]
    return jnp.concatenate(sort_flips(pieces, y)).transpose(1, 0, 2)


def gather_rows(chunk, part, z):
    a3 = move_mirror(part)
    a1 = move_z(a3, 2)
    a2, a0 = move_z(jnp.stack([a3, a1]), 1)
    own = jnp.concatenate(sort_flips((a0, a1, a2, a3), z)).transpose(1, 0, 2)
    return gather_ring(chunk, own, "x")


def gather_ring(chunk, block, axis):
    first, second = flips(chunk)
    pair = jnp.stack([block, move_ring(block, axis, first)])
    return pair, move_ring(pair, axis, second)


def reduce_hidden(chunk, keep, send):
    second, first = flips(chunk)
    other = move_core(send)
    far = move_ring(add(keep[2:], other[2:]).astype(BF), "y", first)
    last = move_ring(add(keep[1], other[1], far[1]).astype(BF), "y", second)
    return add(keep[0], other[0], far[0], last)


def reduce_features(chunk, keep, send):
    second, first = flips(chunk)
    far = move_ring(send, "x", first)
    last = move_ring(add(keep[1], far[1]).astype(BF), "x", second)
    total = add(keep[0], far[0], last)
    far = move_z(total[2:].astype(BF), 1)
    last = move_z(add(total[1], far[1]).astype(BF), 2)
    return add(total[0], far[0], last)


def sum_over_dp(array):
    array = array + move_core(array)
    return array + move_y(array, 1) + move_y(array, 2) + move_y(array, 3)


def per_device(
    loss_sensitivity_outgoing,
    expansion_factor,
    contraction_factor,
    intermediate_affine_values,
    centered_unscaled_entry,
    inverse_spread_per_position,
    layernorm_multiplier,
):
    x, y, z, c = (lax.axis_index(name) for name in ("x", "y", "z", "core"))
    pos = jnp.stack([x, y, z, c]).astype(jnp.int32)
    model = 8 * expansion_factor.shape[1]
    rows = own_features(loss_sensitivity_outgoing[0], y, c)
    slope = slope_rows(intermediate_affine_values[0])

    def by_chunk(array):
        rest = array.shape[1:]
        array = array.reshape(2, 4, CHUNKS, ROWS, *rest)
        array = array.transpose(2, 1, 0, 3, *range(4, array.ndim))
        return array.reshape(CHUNKS, 32, *rest)

    entry = by_chunk(centered_unscaled_entry[0]).astype(F32)
    spread = by_chunk(inverse_spread_per_position[0])
    gain = layernorm_multiplier[0]

    mine, scaled = [], []
    for k in range(CHUNKS):
        gathered = gather_rows(k, rows[ROWS * k : ROWS * (k + 1)], z)
        keep, send, own_rows = hidden_product(k, pos, *gathered, contraction_factor[0])
        block = (reduce_hidden(k, keep, send) * slope[k]).astype(BF)
        near_pair, wide_pair = gather_ring(k, block, "y")
        pairs = (near_pair, wide_pair, move_core(near_pair), move_core(wide_pair))
        keep, send = feature_product(k, pos, pairs, expansion_factor[0])
        mine.append(own_rows.reshape(32, -1))
        scaled.append(gain * reduce_features(k, keep, send))
    scaled = jnp.stack(scaled)
    upstream = jnp.stack(mine)
    sums = sum_over_dp(jnp.stack([jnp.sum(scaled, axis=2), jnp.sum(scaled * entry, axis=2)]))
    result = upstream + spread[:, :, None] * (
        scaled - sums[0][:, :, None] / model - entry * sums[1][:, :, None] / model
    )
    result = result.reshape(CHUNKS, 4, 2, ROWS, -1).transpose(2, 1, 0, 3, 4)
    return result.reshape(1, 96, -1).astype(BF)


def solution(mesh):
    split = Mesh(mesh.devices.reshape(2, 4, 2, 4, 4), ("section", "y", "core", "z", "x"))
    dp, mp = ("y", "core"), ("z", "x")
    in_specs = (
        P("section", dp + mp, None),
        P("section", dp, mp),
        P("section", mp, dp),
        P("section", dp, mp),
        P("section", mp, dp),
        P("section", mp),
        P("section", dp),
    )
    out_specs = P("section", mp, dp)
    return jax.shard_map(per_device, mesh=split, in_specs=in_specs, out_specs=out_specs, check_vma=False)
```

```python
import functools
import math

import jax
import jax.numpy as jnp
from jax import lax
from jax.experimental import pallas as pl
from jax.experimental.pallas import tpu as pltpu
from jax.sharding import Mesh, PartitionSpec as P

BF = jnp.bfloat16
F32 = jnp.float32
CHUNKS = 3
ROWS = 12 // CHUNKS
ORDER = (0, 2, 0, 1, 0, 1, 0, 2, 0, 1, 2, 1, 0, 1, 0, 2, 0, 1, 0, 2, 1, 0, 2, 2, 1, 0, 0, 2, 1, 0, 2, 1, 2, 1, 1, 2, 2, 1, 0, 0, 2, 1, 2, 1, 2, 1, 0, 2)


def near(core):
    return 1 + 2 * core


def wide(core):
    return 3 - 2 * core


def move_ring(array, axis, flip):
    pairs = [(c, i, c, i ^ flip(c)) for c in range(2) for i in range(4)]
    if axis == "y":
        return lax.ppermute(array, ("y", "core"), [(2 * i + c, 2 * j + d) for c, i, d, j in pairs])
    return lax.ppermute(array, ("core", axis), [(4 * c + i, 4 * d + j) for c, i, d, j in pairs])


def move_y(array, flip):
    return lax.ppermute(array, "y", [(y, y ^ flip) for y in range(4)])


def move_z(array, flip):
    return lax.ppermute(array, "z", [(z, z ^ flip) for z in range(4)])


def move_mirror(array):
    return lax.ppermute(array, ("section", "z"), [(i, 7 - i) for i in range(8)])


def move_core(array):
    return lax.ppermute(array, "core", [(0, 1), (1, 0)])


def flips(chunk):
    return (near, wide) if chunk % 2 == 0 else (wide, near)


def ring_order(chunk, core):
    first, second = flips(chunk)
    return 0, first(core), second(core), 2


def gelu_slope(u):
    c = math.sqrt(2.0 / math.pi)
    t = jnp.tanh(c * (u + 0.044715 * u * u * u))
    return 0.5 * (1.0 + t) + 0.5 * u * (1.0 - t * t) * c * (1.0 + 3.0 * 0.044715 * u * u)


def nt_dot(left, right):
    return lax.dot_general(left, right, (((1,), (1,)), ((), ())), preferred_element_type=F32)


def full(shape):
    return pl.BlockSpec(shape, lambda i: (0,) * len(shape))


SMEM = pl.BlockSpec(memory_space=pltpu.SMEM)


def slope_kernel(u, *outs):
    values = gelu_slope(u[...].astype(F32))
    for k in range(CHUNKS):
        pieces = []
        for x in range(4):
            for z in range(4):
                start = (4 * z + x) * 12 + ROWS * k
                pieces.append(values[start : start + ROWS])
        outs[k][...] = jnp.concatenate(pieces, axis=0)


def slope_rows(u):
    rows, width = u.shape
    tile = min(512, width)
    return pl.pallas_call(
        slope_kernel,
        grid=(width // tile,),
        in_specs=[pl.BlockSpec((rows, tile), lambda i: (0, i))],
        out_specs=[pl.BlockSpec((rows // CHUNKS, tile), lambda i: (0, i))] * CHUNKS,
        out_shape=[jax.ShapeDtypeStruct((rows // CHUNKS, width), F32)] * CHUNKS,
        compiler_params=pltpu.CompilerParams(vmem_limit_bytes=16 * 2**20),
        cost_estimate=pl.CostEstimate(flops=20 * rows * width, bytes_accessed=6 * rows * width, transcendentals=rows * width),
    )(u)


def hidden_kernel(chunk, pos, near_pair, wide_pair, weight, keep, send, mine, lhs):
    x, y, z, c = pos[0], pos[1], pos[2], pos[3]

    @pl.when(pl.program_id(0) == 0)
    def _():
        for c_rel in range(2):
            core = jnp.bitwise_xor(c, c_rel)
            for j, flip in enumerate(ring_order(chunk, core)):
                source = 2 * jnp.bitwise_xor(y, flip) + core
                for x_rel, x_flip in enumerate(ring_order(chunk, c)):
                    ref = near_pair if x_rel < 2 else wide_pair
                    lhs[4 * c_rel + j, jnp.bitwise_xor(x, x_flip)] = ref[x_rel % 2, source]
        source = 2 * z + x // 2
        for x_rel, x_flip in enumerate(ring_order(chunk, c)):
            ref = near_pair if x_rel < 2 else wide_pair
            rows = ref[x_rel % 2, source].astype(F32)
            picked = jnp.where(lax.rem(x, 2) == 0, rows[:8], rows[8:])
            mine[jnp.bitwise_xor(x, x_flip)] = picked

    rows = lhs[...].reshape(512, -1)
    product = nt_dot(rows, weight[...]).astype(BF)
    keep[...] = product[:256].reshape(keep.shape)
    send[...] = product[256:].reshape(send.shape)


def hidden_product(chunk, pos, near_pair, wide_pair, weight):
    width, depth = weight.shape
    tile = min(512, width)
    out_block = pl.BlockSpec((4, 64, tile), lambda i: (0, 0, i))
    return pl.pallas_call(
        functools.partial(hidden_kernel, chunk),
        grid=(width // tile,),
        in_specs=[
            SMEM,
            full(near_pair.shape),
            full(wide_pair.shape),
            pl.BlockSpec((tile, depth), lambda i: (i, 0)),
        ],
        out_specs=[out_block, out_block, full((4, 8, depth))],
        out_shape=[
            jax.ShapeDtypeStruct((4, 64, width), BF),
            jax.ShapeDtypeStruct((4, 64, width), BF),
            jax.ShapeDtypeStruct((4, 8, depth), F32),
        ],
        scratch_shapes=[pltpu.VMEM((8, 4, 16, depth), BF)],
        compiler_params=pltpu.CompilerParams(vmem_limit_bytes=16 * 2**20),
        cost_estimate=pl.CostEstimate(
            flops=2 * 512 * width * depth, bytes_accessed=2 * (width * depth + 512 * (width + depth)), transcendentals=0
        ),
    )(pos, near_pair, wide_pair, weight)


def feature_kernel(chunk, pos, near_same, wide_same, near_other, wide_other, weight, keep, send, lhs, result):
    x, y, z, c = pos[0], pos[1], pos[2], pos[3]

    @pl.when(pl.program_id(0) == 0)
    def _():
        for c_rel, (near_pair, wide_pair) in enumerate(((near_same, wide_same), (near_other, wide_other))):
            core = jnp.bitwise_xor(c, c_rel)
            for j, flip in enumerate(ring_order(chunk, core)):
                ref = near_pair if j < 2 else wide_pair
                lhs[2 * jnp.bitwise_xor(y, flip) + core] = ref[j % 2]

    rows = lhs[...].reshape(512, -1)
    result[...] = nt_dot(rows, weight[...]).reshape(result.shape)
    for x_rel, x_flip in enumerate(ring_order(chunk, c)):
        to = jnp.bitwise_xor(x, x_flip)
        out = keep if x_rel < 2 else send
        for z_rel, z_flip in enumerate((0, 2, 1, 3)):
            rows = result[2 * jnp.bitwise_xor(z, z_flip) + to // 2, :, lax.rem(to, 2)]
            out[x_rel % 2, z_rel] = rows.reshape(32, -1).astype(BF)


def feature_product(chunk, pos, pairs, weight):
    width, depth = weight.shape
    tile = min(256, width)
    out_block = pl.BlockSpec((2, 4, 32, tile), lambda i: (0, 0, 0, i))
    return pl.pallas_call(
        functools.partial(feature_kernel, chunk),
        grid=(width // tile,),
        in_specs=[SMEM] + [full(pair.shape) for pair in pairs] + [pl.BlockSpec((tile, depth), lambda i: (i, 0))],
        out_specs=[out_block, out_block],
        out_shape=[jax.ShapeDtypeStruct((2, 4, 32, width), BF)] * 2,
        scratch_shapes=[pltpu.VMEM((8, 64, depth), BF), pltpu.VMEM((8, 4, 2, 8, tile), F32)],
        compiler_params=pltpu.CompilerParams(vmem_limit_bytes=20 * 2**20),
        cost_estimate=pl.CostEstimate(
            flops=2 * 512 * width * depth, bytes_accessed=2 * (width * depth + 512 * (width + depth)), transcendentals=0
        ),
    )(pos, *pairs, weight)


def add(*terms):
    return functools.reduce(jnp.add, [term.astype(F32) for term in terms])


def sort_flips(pieces, at):
    a0, a1, a2, a3 = pieces
    odd, high = at % 2 == 1, at >= 2
    a0, a1 = jnp.where(odd, a1, a0), jnp.where(odd, a0, a1)
    a2, a3 = jnp.where(odd, a3, a2), jnp.where(odd, a2, a3)
    a0, a2 = jnp.where(high, a2, a0), jnp.where(high, a0, a2)
    a1, a3 = jnp.where(high, a3, a1), jnp.where(high, a1, a3)
    return a0, a1, a2, a3


def own_features(rows, y, c):
    depth = rows.shape[1] // 8
    parts = [jnp.stack([rows[:, (2 * i + core) * depth :][:, :depth] for i in range(4)]) for core in range(2)]
    low = c == 0
    mine = jnp.where(low, parts[0], parts[1])
    other = move_core(jnp.where(low, parts[1], parts[0]))
    both = jnp.stack([jnp.where(low, mine, other), jnp.where(low, other, mine)], axis=1)

    def block(flip):
        return lax.dynamic_index_in_dim(both, y ^ flip, 0, keepdims=False)

    pieces = [block(0)] + [move_y(block(flip), flip) for flip in (1, 2, 3)]
    return jnp.concatenate(sort_flips(pieces, y)).transpose(1, 0, 2)


def chunk_steps(k, pos, part, slope, gain, weights):
    x, y, z, c = pos
    pos = jnp.stack(pos).astype(jnp.int32)
    first, second = flips(k)

    (part,) = yield (part,), ()
    (a3,) = yield (move_mirror(part),), (part,)
    (a3, a1) = yield (a3, move_z(a3, 2)), (a3,)
    pair = jnp.stack([a3, a1])
    (pair, moved) = yield (pair, move_z(pair, 1)), (pair,)
    own = jnp.concatenate(sort_flips((moved[1], pair[1], moved[0], pair[0]), z)).transpose(1, 0, 2)
    (own, moved) = yield (own, move_ring(own, "x", first)), (own,)
    pair = jnp.stack([own, moved])
    (pair, moved) = yield (pair, move_ring(pair, "x", second)), (pair,)
    keep, send, mine = hidden_product(k, pos, pair, moved, weights[0])
    (keep, other) = yield (keep, move_core(send)), (send,)
    send = add(keep[2:], other[2:]).astype(BF)
    (keep, other, far) = yield (keep, other, move_ring(send, "y", second)), (send,)
    send = add(keep[1], other[1], far[1]).astype(BF)
    (keep, other, far, last) = yield (keep, other, far, move_ring(send, "y", first)), (send,)
    block = (add(keep[0], other[0], far[0], last) * slope).astype(BF)
    (block, moved) = yield (block, move_ring(block, "y", first)), (block,)
    pair = jnp.stack([block, moved])
    (pair, other, moved) = yield (pair, move_core(pair), move_ring(pair, "y", second)), (pair,)
    (pair, other, moved, moved_other) = yield (pair, other, moved, move_core(moved)), (moved,)
    keep, send = feature_product(k, pos, (pair, moved, other, moved_other), weights[1])
    (keep, far) = yield (keep, move_ring(send, "x", second)), (send,)
    send = add(keep[1], far[1]).astype(BF)
    (keep, far, last) = yield (keep, far, move_ring(send, "x", first)), (send,)
    total = add(keep[0], far[0], last)
    send = total[2:].astype(BF)
    (total, far) = yield (total, move_z(send, 1)), (send,)
    send = add(total[1], far[1]).astype(BF)
    (total, far, last) = yield (total, far, move_z(send, 2)), (send,)
    return mine.reshape(32, -1), gain * add(total[0], far[0], last)


def run_chunks(chunks, order):
    results = [None] * len(chunks)
    waiting = [next(chunk)[0] for chunk in chunks]
    sent = ()
    for k in order:
        ready = lax.optimization_barrier(tuple(waiting[k]) + sent)[: len(waiting[k])]
        try:
            waiting[k], sent = chunks[k].send(ready)
        except StopIteration as stop:
            results[k], sent = stop.value, ()
    return results


def sum_over_dp(array):
    array = array + move_core(array)
    return array + move_y(array, 1) + move_y(array, 2) + move_y(array, 3)


def per_device(
    loss_sensitivity_outgoing,
    expansion_factor,
    contraction_factor,
    intermediate_affine_values,
    centered_unscaled_entry,
    inverse_spread_per_position,
    layernorm_multiplier,
):
    x, y, z, c = (lax.axis_index(name) for name in ("x", "y", "z", "core"))
    model = 8 * expansion_factor.shape[1]
    rows = own_features(loss_sensitivity_outgoing[0], y, c)
    slope = slope_rows(intermediate_affine_values[0])

    def by_chunk(array):
        rest = array.shape[1:]
        array = array.reshape(2, 4, CHUNKS, ROWS, *rest)
        array = array.transpose(2, 1, 0, 3, *range(4, array.ndim))
        return array.reshape(CHUNKS, 32, *rest)

    entry = by_chunk(centered_unscaled_entry[0]).astype(F32)
    spread = by_chunk(inverse_spread_per_position[0])
    gain = layernorm_multiplier[0]

    chunks = [
        chunk_steps(
            k,
            (x, y, z, c),
            rows[ROWS * k : ROWS * (k + 1)],
            slope[k],
            gain,
            (contraction_factor[0], expansion_factor[0]),
        )
        for k in range(CHUNKS)
    ]
    mine, scaled = zip(*run_chunks(chunks, ORDER))
    scaled = jnp.stack(scaled)
    upstream = jnp.stack(mine)
    sums = sum_over_dp(jnp.stack([jnp.sum(scaled, axis=2), jnp.sum(scaled * entry, axis=2)]))
    result = upstream + spread[:, :, None] * (
        scaled - sums[0][:, :, None] / model - entry * sums[1][:, :, None] / model
    )
    result = result.reshape(CHUNKS, 4, 2, ROWS, -1).transpose(2, 1, 0, 3, 4)
    return result.reshape(1, 96, -1).astype(BF)


def solution(mesh):
    split = Mesh(mesh.devices.reshape(2, 4, 2, 4, 4), ("section", "y", "core", "z", "x"))
    dp, mp = ("y", "core"), ("z", "x")
    in_specs = (
        P("section", dp + mp, None),
        P("section", dp, mp),
        P("section", mp, dp),
        P("section", dp, mp),
        P("section", mp, dp),
        P("section", mp),
        P("section", dp),
    )
    out_specs = P("section", mp, dp)
    return jax.shard_map(per_device, mesh=split, in_specs=in_specs, out_specs=out_specs, check_vma=False)
```

```python
import functools
import math

import jax
import jax.numpy as jnp
from jax import lax
from jax.experimental import pallas as pl
from jax.experimental.pallas import tpu as pltpu
from jax.sharding import Mesh, PartitionSpec as P

BF = jnp.bfloat16
F32 = jnp.float32
CHUNKS = 3
ROWS = 12 // CHUNKS


def near(core):
    return 1 + 2 * core


def wide(core):
    return 3 - 2 * core


def move_ring(array, axis, flip):
    pairs = [(c, i, c, i ^ flip(c)) for c in range(2) for i in range(4)]
    if axis == "y":
        return lax.ppermute(array, ("y", "core"), [(2 * i + c, 2 * j + d) for c, i, d, j in pairs])
    return lax.ppermute(array, ("core", axis), [(4 * c + i, 4 * d + j) for c, i, d, j in pairs])


def move_y(array, flip):
    return lax.ppermute(array, "y", [(y, y ^ flip) for y in range(4)])


def move_z(array, flip):
    return lax.ppermute(array, "z", [(z, z ^ flip) for z in range(4)])


def move_mirror(array, flip):
    devices = [(s, y, z) for s in range(2) for y in range(4) for z in range(4)]
    pairs = [(16 * s + 4 * y + z, 16 * (1 - s) + 4 * (y ^ flip) + 3 - z) for s, y, z in devices]
    return lax.ppermute(array, ("section", "y", "z"), pairs)


def move_core(array):
    return lax.ppermute(array, "core", [(0, 1), (1, 0)])


def flips(chunk):
    return (near, wide) if chunk % 2 == 0 else (wide, near)


def ring_order(chunk, core):
    first, second = flips(chunk)
    return 0, first(core), second(core), 2


def gelu_slope(u):
    c = math.sqrt(2.0 / math.pi)
    t = jnp.tanh(c * (u + 0.044715 * u * u * u))
    return 0.5 * (1.0 + t) + 0.5 * u * (1.0 - t * t) * c * (1.0 + 3.0 * 0.044715 * u * u)


def nt_dot(left, right):
    return lax.dot_general(left, right, (((1,), (1,)), ((), ())), preferred_element_type=F32)


def full(shape):
    return pl.BlockSpec(shape, lambda i: (0,) * len(shape))


SMEM = pl.BlockSpec(memory_space=pltpu.SMEM)


def slope_kernel(u, *outs):
    values = gelu_slope(u[...].astype(F32))
    for k in range(CHUNKS):
        pieces = []
        for x in range(4):
            for z in range(4):
                start = (4 * z + x) * 12 + ROWS * k
                pieces.append(values[start : start + ROWS])
        outs[k][...] = jnp.concatenate(pieces, axis=0)


def slope_rows(u):
    rows, width = u.shape
    tile = min(512, width)
    return pl.pallas_call(
        slope_kernel,
        grid=(width // tile,),
        in_specs=[pl.BlockSpec((rows, tile), lambda i: (0, i))],
        out_specs=[pl.BlockSpec((rows // CHUNKS, tile), lambda i: (0, i))] * CHUNKS,
        out_shape=[jax.ShapeDtypeStruct((rows // CHUNKS, width), F32)] * CHUNKS,
        compiler_params=pltpu.CompilerParams(vmem_limit_bytes=16 * 2**20),
        cost_estimate=pl.CostEstimate(flops=20 * rows * width, bytes_accessed=6 * rows * width, transcendentals=rows * width),
    )(u)


def hidden_kernel(chunk, pos, near_pair, wide_pair, weight, keep, send, mine, lhs):
    x, y, z, c = pos[0], pos[1], pos[2], pos[3]

    @pl.when(pl.program_id(0) == 0)
    def _():
        for c_rel in range(2):
            core = jnp.bitwise_xor(c, c_rel)
            for j, flip in enumerate(ring_order(chunk, core)):
                source = 2 * jnp.bitwise_xor(y, flip) + core
                for x_rel, x_flip in enumerate(ring_order(chunk, c)):
                    ref = near_pair if x_rel < 2 else wide_pair
                    lhs[4 * c_rel + j, jnp.bitwise_xor(x, x_flip)] = ref[x_rel % 2, source]
        source = 2 * z + x // 2
        for x_rel, x_flip in enumerate(ring_order(chunk, c)):
            ref = near_pair if x_rel < 2 else wide_pair
            rows = ref[x_rel % 2, source].astype(F32)
            picked = jnp.where(lax.rem(x, 2) == 0, rows[:8], rows[8:])
            mine[jnp.bitwise_xor(x, x_flip)] = picked

    rows = lhs[...].reshape(512, -1)
    product = nt_dot(rows, weight[...]).astype(BF)
    keep[...] = product[:256].reshape(keep.shape)
    send[...] = product[256:].reshape(send.shape)


def hidden_product(chunk, pos, near_pair, wide_pair, weight):
    width, depth = weight.shape
    tile = min(512, width)
    out_block = pl.BlockSpec((4, 64, tile), lambda i: (0, 0, i))
    return pl.pallas_call(
        functools.partial(hidden_kernel, chunk),
        grid=(width // tile,),
        in_specs=[
            SMEM,
            full(near_pair.shape),
            full(wide_pair.shape),
            pl.BlockSpec((tile, depth), lambda i: (i, 0)),
        ],
        out_specs=[out_block, out_block, full((4, 8, depth))],
        out_shape=[
            jax.ShapeDtypeStruct((4, 64, width), BF),
            jax.ShapeDtypeStruct((4, 64, width), BF),
            jax.ShapeDtypeStruct((4, 8, depth), F32),
        ],
        scratch_shapes=[pltpu.VMEM((8, 4, 16, depth), BF)],
        compiler_params=pltpu.CompilerParams(vmem_limit_bytes=16 * 2**20),
        cost_estimate=pl.CostEstimate(
            flops=2 * 512 * width * depth, bytes_accessed=2 * (width * depth + 512 * (width + depth)), transcendentals=0
        ),
    )(pos, near_pair, wide_pair, weight)


def feature_kernel(chunk, pos, near_same, wide_same, near_other, wide_other, weight, keep, send, lhs, result):
    x, y, z, c = pos[0], pos[1], pos[2], pos[3]

    @pl.when(pl.program_id(0) == 0)
    def _():
        for c_rel, (near_pair, wide_pair) in enumerate(((near_same, wide_same), (near_other, wide_other))):
            core = jnp.bitwise_xor(c, c_rel)
            for j, flip in enumerate(ring_order(chunk, core)):
                ref = near_pair if j < 2 else wide_pair
                lhs[2 * jnp.bitwise_xor(y, flip) + core] = ref[j % 2]

    rows = lhs[...].reshape(512, -1)
    result[...] = nt_dot(rows, weight[...]).reshape(result.shape)
    for x_rel, x_flip in enumerate(ring_order(chunk, c)):
        to = jnp.bitwise_xor(x, x_flip)
        out = keep if x_rel < 2 else send
        for z_rel, z_flip in enumerate((0, 2, 1, 3)):
            rows = result[2 * jnp.bitwise_xor(z, z_flip) + to // 2, :, lax.rem(to, 2)]
            out[x_rel % 2, z_rel] = rows.reshape(32, -1).astype(BF)


def feature_product(chunk, pos, pairs, weight):
    width, depth = weight.shape
    tile = min(256, width)
    out_block = pl.BlockSpec((2, 4, 32, tile), lambda i: (0, 0, 0, i))
    return pl.pallas_call(
        functools.partial(feature_kernel, chunk),
        grid=(width // tile,),
        in_specs=[SMEM] + [full(pair.shape) for pair in pairs] + [pl.BlockSpec((tile, depth), lambda i: (i, 0))],
        out_specs=[out_block, out_block],
        out_shape=[jax.ShapeDtypeStruct((2, 4, 32, width), BF)] * 2,
        scratch_shapes=[pltpu.VMEM((8, 64, depth), BF), pltpu.VMEM((8, 4, 2, 8, tile), F32)],
        compiler_params=pltpu.CompilerParams(vmem_limit_bytes=20 * 2**20),
        cost_estimate=pl.CostEstimate(
            flops=2 * 512 * width * depth, bytes_accessed=2 * (width * depth + 512 * (width + depth)), transcendentals=0
        ),
    )(pos, *pairs, weight)


def add(*terms):
    return functools.reduce(jnp.add, [term.astype(F32) for term in terms])


def sort_flips(pieces, at):
    a0, a1, a2, a3 = pieces
    odd, high = at % 2 == 1, at >= 2
    a0, a1 = jnp.where(odd, a1, a0), jnp.where(odd, a0, a1)
    a2, a3 = jnp.where(odd, a3, a2), jnp.where(odd, a2, a3)
    a0, a2 = jnp.where(high, a2, a0), jnp.where(high, a0, a2)
    a1, a3 = jnp.where(high, a3, a1), jnp.where(high, a1, a3)
    return a0, a1, a2, a3


def mirrored_features(rows, y, c):
    depth = rows.shape[1] // 8
    parts = [jnp.stack([rows[:, (2 * i + core) * depth :][:, :depth] for i in range(4)]) for core in range(2)]
    low = c == 0
    mine = jnp.where(low, parts[0], parts[1])
    other = move_core(jnp.where(low, parts[1], parts[0]))
    both = jnp.stack([jnp.where(low, mine, other), jnp.where(low, other, mine)], axis=1)

    def block(flip):
        return lax.dynamic_index_in_dim(both, y ^ flip, 0, keepdims=False)

    pieces = [move_mirror(block(flip), flip) for flip in range(4)]
    return jnp.concatenate(sort_flips(pieces, y)).transpose(1, 0, 2)


def gather_rows(rows, z):
    a1 = move_z(rows, 2)
    a2, a0 = move_z(jnp.stack([rows, a1]), 1)
    rows = jnp.stack(sort_flips((a0, a1, a2, rows), z))
    parts = [rows[:, ROWS * k : ROWS * (k + 1)].reshape(4 * ROWS, 8, -1) for k in range(CHUNKS)]
    return [part.transpose(1, 0, 2) for part in parts]


def gather_ring(chunk, block, axis):
    first, second = flips(chunk)
    pair = jnp.stack([block, move_ring(block, axis, first)])
    return pair, move_ring(pair, axis, second)


def reduce_hidden(chunk, keep, other, send):
    second, first = flips(chunk)
    far = move_ring(send, "y", first)
    last = move_ring(add(keep[1], other[1], far[1]).astype(BF), "y", second)
    return add(keep[0], other[0], far[0], last)


def reduce_features(chunk, keep, send):
    second, first = flips(chunk)
    far = move_ring(send, "x", first)
    last = move_ring(add(keep[1], far[1]).astype(BF), "x", second)
    total = add(keep[0], far[0], last)
    far = move_z(total[2:].astype(BF), 1)
    last = move_z(add(total[1], far[1]).astype(BF), 2)
    return add(total[0], far[0], last)


def sum_over_dp(array):
    array = array + move_core(array)
    return array + move_y(array, 1) + move_y(array, 2) + move_y(array, 3)


def per_device(
    loss_sensitivity_outgoing,
    expansion_factor,
    contraction_factor,
    intermediate_affine_values,
    centered_unscaled_entry,
    inverse_spread_per_position,
    layernorm_multiplier,
):
    x, y, z, c = (lax.axis_index(name) for name in ("x", "y", "z", "core"))
    pos = jnp.stack([x, y, z, c]).astype(jnp.int32)
    model = 8 * expansion_factor.shape[1]
    rows = mirrored_features(loss_sensitivity_outgoing[0], y, c)
    slope = slope_rows(intermediate_affine_values[0])

    def by_chunk(array):
        rest = array.shape[1:]
        array = array.reshape(2, 4, CHUNKS, ROWS, *rest)
        array = array.transpose(2, 1, 0, 3, *range(4, array.ndim))
        return array.reshape(CHUNKS, 32, *rest)

    entry = by_chunk(centered_unscaled_entry[0]).astype(F32)
    spread = by_chunk(inverse_spread_per_position[0])
    gain = layernorm_multiplier[0]

    rows, slope = lax.optimization_barrier((rows, slope))
    parts = gather_rows(rows, z)
    moved = [move_ring(parts[k], "x", flips(k)[0]) for k in range(CHUNKS)]
    moved = lax.optimization_barrier(moved)
    near_pairs = [jnp.stack([parts[k], moved[k]]) for k in range(CHUNKS)]
    wide_pairs = [move_ring(near_pairs[k], "x", flips(k)[1]) for k in range(CHUNKS)]
    mine, halves = [], []
    for k in range(CHUNKS):
        keep, send, own_rows = hidden_product(k, pos, near_pairs[k], wide_pairs[k], contraction_factor[0])
        other = move_core(send)
        mine.append(own_rows.reshape(32, -1))
        halves.append((keep, other, add(keep[2:], other[2:]).astype(BF)))
    scaled = []
    for k in range(CHUNKS):
        block = (reduce_hidden(k, *halves[k]) * slope[k]).astype(BF)
        near_pair, wide_pair = gather_ring(k, block, "y")
        pairs = (near_pair, wide_pair, move_core(near_pair), move_core(wide_pair))
        keep, send = feature_product(k, pos, pairs, expansion_factor[0])
        scaled.append(gain * reduce_features(k, keep, send))
    scaled = jnp.stack(scaled)
    upstream = jnp.stack(mine)
    sums = sum_over_dp(jnp.stack([jnp.sum(scaled, axis=2), jnp.sum(scaled * entry, axis=2)]))
    result = upstream + spread[:, :, None] * (
        scaled - sums[0][:, :, None] / model - entry * sums[1][:, :, None] / model
    )
    result = result.reshape(CHUNKS, 4, 2, ROWS, -1).transpose(2, 1, 0, 3, 4)
    return result.reshape(1, 96, -1).astype(BF)


def solution(mesh):
    split = Mesh(mesh.devices.reshape(2, 4, 2, 4, 4), ("section", "y", "core", "z", "x"))
    dp, mp = ("y", "core"), ("z", "x")
    in_specs = (
        P("section", dp + mp, None),
        P("section", dp, mp),
        P("section", mp, dp),
        P("section", dp, mp),
        P("section", mp, dp),
        P("section", mp),
        P("section", dp),
    )
    out_specs = P("section", mp, dp)
    return jax.shard_map(per_device, mesh=split, in_specs=in_specs, out_specs=out_specs, check_vma=False)
```

```python
import functools
import math

import jax
import jax.numpy as jnp
from jax import lax
from jax.experimental import pallas as pl
from jax.experimental.pallas import tpu as pltpu
from jax.sharding import Mesh, PartitionSpec as P

BF = jnp.bfloat16
F32 = jnp.float32
CHUNKS = 3
ROWS = 12 // CHUNKS


def near(core):
    return 1 + 2 * core


def wide(core):
    return 3 - 2 * core


def move_ring(array, axis, flip):
    pairs = [(c, i, c, i ^ flip(c)) for c in range(2) for i in range(4)]
    if axis == "y":
        return lax.ppermute(array, ("y", "core"), [(2 * i + c, 2 * j + d) for c, i, d, j in pairs])
    return lax.ppermute(array, ("core", axis), [(4 * c + i, 4 * d + j) for c, i, d, j in pairs])


def move_y(array, flip):
    return lax.ppermute(array, "y", [(y, y ^ flip) for y in range(4)])


def move_z(array, flip):
    return lax.ppermute(array, "z", [(z, z ^ flip) for z in range(4)])


def move_mirror(array):
    return lax.ppermute(array, ("section", "z"), [(i, 7 - i) for i in range(8)])


def move_core(array):
    return lax.ppermute(array, "core", [(0, 1), (1, 0)])


def flips(chunk):
    return (near, wide) if chunk % 2 == 0 else (wide, near)


def crossed(chunk):
    return chunk == CHUNKS - 1


Z_ORDER = 0, 2, 1, 3
MIRRORED_Z_ORDER = 3, 1, 2, 0


def ring_order(chunk, core):
    first, second = flips(chunk)
    return 0, first(core), second(core), 2


def gelu_slope(u):
    c = math.sqrt(2.0 / math.pi)
    t = jnp.tanh(c * (u + 0.044715 * u * u * u))
    return 0.5 * (1.0 + t) + 0.5 * u * (1.0 - t * t) * c * (1.0 + 3.0 * 0.044715 * u * u)


def nt_dot(left, right):
    return lax.dot_general(left, right, (((1,), (1,)), ((), ())), preferred_element_type=F32)


def full(shape):
    return pl.BlockSpec(shape, lambda i: (0,) * len(shape))


SMEM = pl.BlockSpec(memory_space=pltpu.SMEM)


def slope_kernel(u, *outs):
    values = gelu_slope(u[...].astype(F32))
    for k in range(CHUNKS):
        pieces = []
        for outer in range(4):
            for inner in range(4):
                z, x = (outer, inner) if crossed(k) else (inner, outer)
                start = (4 * z + x) * 12 + ROWS * k
                pieces.append(values[start : start + ROWS])
        outs[k][...] = jnp.concatenate(pieces, axis=0)


def slope_rows(u):
    rows, width = u.shape
    tile = min(512, width)
    return pl.pallas_call(
        slope_kernel,
        grid=(width // tile,),
        in_specs=[pl.BlockSpec((rows, tile), lambda i: (0, i))],
        out_specs=[pl.BlockSpec((rows // CHUNKS, tile), lambda i: (0, i))] * CHUNKS,
        out_shape=[jax.ShapeDtypeStruct((rows // CHUNKS, width), F32)] * CHUNKS,
        compiler_params=pltpu.CompilerParams(vmem_limit_bytes=16 * 2**20),
        cost_estimate=pl.CostEstimate(flops=20 * rows * width, bytes_accessed=6 * rows * width, transcendentals=rows * width),
    )(u)


def hidden_kernel(chunk, pos, near_pair, wide_pair, weight, keep, send, mine, lhs):
    x, y, z, c = pos[0], pos[1], pos[2], pos[3]

    @pl.when(pl.program_id(0) == 0)
    def _():
        at, order = (z, MIRRORED_Z_ORDER) if crossed(chunk) else (x, ring_order(chunk, c))
        for c_rel in range(2):
            core = jnp.bitwise_xor(c, c_rel)
            for j, flip in enumerate(ring_order(chunk, core)):
                source = 2 * jnp.bitwise_xor(y, flip) + core
                for rel, rel_flip in enumerate(order):
                    ref = near_pair if rel < 2 else wide_pair
                    lhs[4 * c_rel + j, jnp.bitwise_xor(at, rel_flip)] = ref[rel % 2, source]
        source = 2 * z + x // 2
        for rel, rel_flip in enumerate(order):
            ref = near_pair if rel < 2 else wide_pair
            rows = ref[rel % 2, source].astype(F32)
            origin = jnp.bitwise_xor(at, rel_flip)
            if crossed(chunk):

                @pl.when(origin // 2 == lax.rem(x, 2))
                def _(rows=rows, origin=origin):
                    mine[pl.ds(2 * lax.rem(origin, 2), 2)] = rows.reshape(2, 8, -1)

            else:
                mine[origin] = jnp.where(lax.rem(x, 2) == 0, rows[:8], rows[8:])

    rows = lhs[...].reshape(512, -1)
    product = nt_dot(rows, weight[...]).astype(BF)
    keep[...] = product[:256].reshape(keep.shape)
    send[...] = product[256:].reshape(send.shape)


def hidden_product(chunk, pos, near_pair, wide_pair, weight):
    width, depth = weight.shape
    tile = min(512, width)
    out_block = pl.BlockSpec((4, 64, tile), lambda i: (0, 0, i))
    return pl.pallas_call(
        functools.partial(hidden_kernel, chunk),
        grid=(width // tile,),
        in_specs=[
            SMEM,
            full(near_pair.shape),
            full(wide_pair.shape),
            pl.BlockSpec((tile, depth), lambda i: (i, 0)),
        ],
        out_specs=[out_block, out_block, full((4, 8, depth))],
        out_shape=[
            jax.ShapeDtypeStruct((4, 64, width), BF),
            jax.ShapeDtypeStruct((4, 64, width), BF),
            jax.ShapeDtypeStruct((4, 8, depth), F32),
        ],
        scratch_shapes=[pltpu.VMEM((8, 4, 16, depth), BF)],
        compiler_params=pltpu.CompilerParams(vmem_limit_bytes=16 * 2**20),
        cost_estimate=pl.CostEstimate(
            flops=2 * 512 * width * depth, bytes_accessed=2 * (width * depth + 512 * (width + depth)), transcendentals=0
        ),
    )(pos, near_pair, wide_pair, weight)


def feature_kernel(chunk, pos, near_same, wide_same, near_other, wide_other, weight, keep, send, lhs, result):
    x, y, z, c = pos[0], pos[1], pos[2], pos[3]

    @pl.when(pl.program_id(0) == 0)
    def _():
        for c_rel, (near_pair, wide_pair) in enumerate(((near_same, wide_same), (near_other, wide_other))):
            core = jnp.bitwise_xor(c, c_rel)
            for j, flip in enumerate(ring_order(chunk, core)):
                ref = near_pair if j < 2 else wide_pair
                lhs[2 * jnp.bitwise_xor(y, flip) + core] = ref[j % 2]

    rows = lhs[...].reshape(512, -1)
    result[...] = nt_dot(rows, weight[...]).reshape(result.shape)
    for x_rel, x_flip in enumerate(ring_order(chunk, c)):
        to = jnp.bitwise_xor(x, x_flip)
        for z_rel, z_flip in enumerate(Z_ORDER):
            source = 2 * jnp.bitwise_xor(z, z_flip) + to // 2
            if crossed(chunk):
                out = keep if z_rel < 2 else send
                out[z_rel % 2, x_rel] = result[source, lax.rem(to, 2)].astype(BF)
            else:
                out = keep if x_rel < 2 else send
                rows = result[source, :, lax.rem(to, 2)]
                out[x_rel % 2, z_rel] = rows.reshape(32, -1).astype(BF)


def feature_product(chunk, pos, pairs, weight):
    width, depth = weight.shape
    tile = min(256, width)
    out_block = pl.BlockSpec((2, 4, 32, tile), lambda i: (0, 0, 0, i))
    return pl.pallas_call(
        functools.partial(feature_kernel, chunk),
        grid=(width // tile,),
        in_specs=[SMEM] + [full(pair.shape) for pair in pairs] + [pl.BlockSpec((tile, depth), lambda i: (i, 0))],
        out_specs=[out_block, out_block],
        out_shape=[jax.ShapeDtypeStruct((2, 4, 32, width), BF)] * 2,
        scratch_shapes=[
            pltpu.VMEM((8, 64, depth), BF),
            pltpu.VMEM((8, 2, 32, tile) if crossed(chunk) else (8, 4, 2, 8, tile), F32),
        ],
        compiler_params=pltpu.CompilerParams(vmem_limit_bytes=20 * 2**20),
        cost_estimate=pl.CostEstimate(
            flops=2 * 512 * width * depth, bytes_accessed=2 * (width * depth + 512 * (width + depth)), transcendentals=0
        ),
    )(pos, *pairs, weight)


def add(*terms):
    return functools.reduce(jnp.add, [term.astype(F32) for term in terms])


def sort_flips(pieces, at):
    a0, a1, a2, a3 = pieces
    odd, high = at % 2 == 1, at >= 2
    a0, a1 = jnp.where(odd, a1, a0), jnp.where(odd, a0, a1)
    a2, a3 = jnp.where(odd, a3, a2), jnp.where(odd, a2, a3)
    a0, a2 = jnp.where(high, a2, a0), jnp.where(high, a0, a2)
    a1, a3 = jnp.where(high, a3, a1), jnp.where(high, a1, a3)
    return a0, a1, a2, a3


def own_features(rows, y, c):
    depth = rows.shape[1] // 8
    parts = [jnp.stack([rows[:, (2 * i + core) * depth :][:, :depth] for i in range(4)]) for core in range(2)]
    low = c == 0
    mine = jnp.where(low, parts[0], parts[1])
    other = move_core(jnp.where(low, parts[1], parts[0]))
    both = jnp.stack([jnp.where(low, mine, other), jnp.where(low, other, mine)], axis=1)

    def block(flip):
        return lax.dynamic_index_in_dim(both, y ^ flip, 0, keepdims=False)

    pieces = [block(0)] + [move_y(block(flip), flip) for flip in (1, 2, 3)]
    return jnp.concatenate(sort_flips(pieces, y)).transpose(1, 0, 2)


def gather_rows(chunk, part, x, z, c):
    part = move_mirror(part)
    if crossed(chunk):
        pair, (b, e) = gather_ring(chunk, part, "x")
        low = (c + chunk) % 2 == 0
        pieces = part, jnp.where(low, pair[1], b), e, jnp.where(low, b, pair[1])
        own = jnp.concatenate(sort_flips(pieces, x)).transpose(1, 0, 2)
        pair = jnp.stack([own, move_z(own, 2)])
        return pair, move_z(pair, 1)
    a1 = move_z(part, 2)
    a2, a0 = move_z(jnp.stack([part, a1]), 1)
    own = jnp.concatenate(sort_flips((a0, a1, a2, part), z)).transpose(1, 0, 2)
    return gather_ring(chunk, own, "x")


def gather_ring(chunk, block, axis):
    first, second = flips(chunk)
    pair = jnp.stack([block, move_ring(block, axis, first)])
    return pair, move_ring(pair, axis, second)


def reduce_hidden(chunk, keep, send):
    second, first = flips(chunk)
    other = move_core(send)
    far = move_ring(add(keep[2:], other[2:]).astype(BF), "y", first)
    last = move_ring(add(keep[1], other[1], far[1]).astype(BF), "y", second)
    return add(keep[0], other[0], far[0], last)


def reduce_ring(chunk, keep, send):
    second, first = flips(chunk)
    far = move_ring(send, "x", first)
    last = move_ring(add(keep[1], far[1]).astype(BF), "x", second)
    return add(keep[0], far[0], last)


def reduce_z(keep, send):
    far = move_z(send, 1)
    last = move_z(add(keep[1], far[1]).astype(BF), 2)
    return add(keep[0], far[0], last)


def reduce_features(chunk, keep, send):
    if crossed(chunk):
        total = reduce_z(keep, send)
        return reduce_ring(chunk, total[:2], total[2:].astype(BF))
    total = reduce_ring(chunk, keep, send)
    return reduce_z(total[:2], total[2:].astype(BF))


def sum_over_dp(array):
    array = array + move_core(array)
    return array + move_y(array, 1) + move_y(array, 2) + move_y(array, 3)


def per_device(
    loss_sensitivity_outgoing,
    expansion_factor,
    contraction_factor,
    intermediate_affine_values,
    centered_unscaled_entry,
    inverse_spread_per_position,
    layernorm_multiplier,
):
    x, y, z, c = (lax.axis_index(name) for name in ("x", "y", "z", "core"))
    pos = jnp.stack([x, y, z, c]).astype(jnp.int32)
    model = 8 * expansion_factor.shape[1]
    rows = own_features(loss_sensitivity_outgoing[0], y, c)
    slope = slope_rows(intermediate_affine_values[0])

    def by_chunk(array):
        array = array.reshape(2, 4, CHUNKS, ROWS, *array.shape[1:])
        parts = [array[:, :, k] if crossed(k) else array[:, :, k].swapaxes(0, 1) for k in range(CHUNKS)]
        return jnp.stack([part.reshape(32, *part.shape[3:]) for part in parts])

    entry = by_chunk(centered_unscaled_entry[0]).astype(F32)
    spread = by_chunk(inverse_spread_per_position[0])
    gain = layernorm_multiplier[0]

    mine, scaled = [], []
    for k in range(CHUNKS):
        gathered = gather_rows(k, rows[ROWS * k : ROWS * (k + 1)], x, z, c)
        keep, send, own_rows = hidden_product(k, pos, *gathered, contraction_factor[0])
        block = (reduce_hidden(k, keep, send) * slope[k]).astype(BF)
        near_pair, wide_pair = gather_ring(k, block, "y")
        pairs = (near_pair, wide_pair, move_core(near_pair), move_core(wide_pair))
        keep, send = feature_product(k, pos, pairs, expansion_factor[0])
        mine.append(own_rows.reshape(32, -1))
        scaled.append(gain * reduce_features(k, keep, send))
    scaled = jnp.stack(scaled)
    upstream = jnp.stack(mine)
    sums = sum_over_dp(jnp.stack([jnp.sum(scaled, axis=2), jnp.sum(scaled * entry, axis=2)]))
    result = upstream + spread[:, :, None] * (
        scaled - sums[0][:, :, None] / model - entry * sums[1][:, :, None] / model
    )
    parts = [
        result[k].reshape(2, 4, ROWS, -1) if crossed(k) else result[k].reshape(4, 2, ROWS, -1).swapaxes(0, 1)
        for k in range(CHUNKS)
    ]
    return jnp.stack(parts, axis=2).reshape(1, 96, -1).astype(BF)


def solution(mesh):
    split = Mesh(mesh.devices.reshape(2, 4, 2, 4, 4), ("section", "y", "core", "z", "x"))
    dp, mp = ("y", "core"), ("z", "x")
    in_specs = (
        P("section", dp + mp, None),
        P("section", dp, mp),
        P("section", mp, dp),
        P("section", dp, mp),
        P("section", mp, dp),
        P("section", mp),
        P("section", dp),
    )
    out_specs = P("section", mp, dp)
    return jax.shard_map(per_device, mesh=split, in_specs=in_specs, out_specs=out_specs, check_vma=False)
```

```python
import functools
import math

import jax
import jax.numpy as jnp
from jax import lax
from jax.experimental import pallas as pl
from jax.experimental.pallas import tpu as pltpu
from jax.sharding import Mesh, PartitionSpec as P

BF = jnp.bfloat16
F32 = jnp.float32
COUNTS = 4, 8
STARTS = 0, 4


def near(core):
    return 1 + 2 * core


def wide(core):
    return 3 - 2 * core


def move_ring(array, axis, flip):
    pairs = [(c, i, c, i ^ flip(c)) for c in range(2) for i in range(4)]
    if axis == "y":
        return lax.ppermute(array, ("y", "core"), [(2 * i + c, 2 * j + d) for c, i, d, j in pairs])
    return lax.ppermute(array, ("core", axis), [(4 * c + i, 4 * d + j) for c, i, d, j in pairs])


def move_y(array, flip):
    return lax.ppermute(array, "y", [(y, y ^ flip) for y in range(4)])


def move_z(array, flip):
    return lax.ppermute(array, "z", [(z, z ^ flip) for z in range(4)])


def move_mirror(array):
    return lax.ppermute(array, ("section", "z"), [(i, 7 - i) for i in range(8)])


def move_core(array):
    return lax.ppermute(array, "core", [(0, 1), (1, 0)])


def flips(chunk):
    return (near, wide) if chunk % 2 == 0 else (wide, near)


def ring_order(chunk, core):
    first, second = flips(chunk)
    return 0, first(core), second(core), 2


def gelu_slope(u):
    c = math.sqrt(2.0 / math.pi)
    t = jnp.tanh(c * (u + 0.044715 * u * u * u))
    return 0.5 * (1.0 + t) + 0.5 * u * (1.0 - t * t) * c * (1.0 + 3.0 * 0.044715 * u * u)


def nt_dot(left, right):
    return lax.dot_general(left, right, (((1,), (1,)), ((), ())), preferred_element_type=F32)


def full(shape):
    return pl.BlockSpec(shape, lambda i: (0,) * len(shape))


SMEM = pl.BlockSpec(memory_space=pltpu.SMEM)


def slope_kernel(u, *outs):
    values = gelu_slope(u[...].astype(F32))
    for k, count in enumerate(COUNTS):
        pieces = []
        for x in range(4):
            for z in range(4):
                start = (4 * z + x) * 12 + STARTS[k]
                pieces.append(values[start : start + count])
        outs[k][...] = jnp.concatenate(pieces, axis=0)


def slope_rows(u):
    rows, width = u.shape
    tile = min(512, width)
    return pl.pallas_call(
        slope_kernel,
        grid=(width // tile,),
        in_specs=[pl.BlockSpec((rows, tile), lambda i: (0, i))],
        out_specs=[pl.BlockSpec((16 * count, tile), lambda i: (0, i)) for count in COUNTS],
        out_shape=[jax.ShapeDtypeStruct((16 * count, width), F32) for count in COUNTS],
        compiler_params=pltpu.CompilerParams(vmem_limit_bytes=16 * 2**20),
        cost_estimate=pl.CostEstimate(flops=20 * rows * width, bytes_accessed=6 * rows * width, transcendentals=rows * width),
    )(u)


def hidden_kernel(chunk, pos, near_pair, wide_pair, weight, keep, send, mine, lhs):
    x, y, z, c = pos[0], pos[1], pos[2], pos[3]

    @pl.when(pl.program_id(0) == 0)
    def _():
        for c_rel in range(2):
            core = jnp.bitwise_xor(c, c_rel)
            for j, flip in enumerate(ring_order(chunk, core)):
                source = 2 * jnp.bitwise_xor(y, flip) + core
                for x_rel, x_flip in enumerate(ring_order(chunk, c)):
                    ref = near_pair if x_rel < 2 else wide_pair
                    lhs[4 * c_rel + j, jnp.bitwise_xor(x, x_flip)] = ref[x_rel % 2, source]
        source = 2 * z + x // 2
        for x_rel, x_flip in enumerate(ring_order(chunk, c)):
            ref = near_pair if x_rel < 2 else wide_pair
            rows = ref[x_rel % 2, source].astype(F32)
            half = rows.shape[0] // 2
            picked = jnp.where(lax.rem(x, 2) == 0, rows[:half], rows[half:])
            mine[jnp.bitwise_xor(x, x_flip)] = picked

    rows = lhs[...].reshape(-1, lhs.shape[-1])
    product = nt_dot(rows, weight[...]).astype(BF)
    half = rows.shape[0] // 2
    keep[...] = product[:half].reshape(keep.shape)
    send[...] = product[half:].reshape(send.shape)


def hidden_product(chunk, pos, near_pair, wide_pair, weight):
    width, depth = weight.shape
    tile = min(512, width)
    count = COUNTS[chunk]
    out_block = pl.BlockSpec((4, 16 * count, tile), lambda i: (0, 0, i))
    return pl.pallas_call(
        functools.partial(hidden_kernel, chunk),
        grid=(width // tile,),
        in_specs=[
            SMEM,
            full(near_pair.shape),
            full(wide_pair.shape),
            pl.BlockSpec((tile, depth), lambda i: (i, 0)),
        ],
        out_specs=[out_block, out_block, full((4, 2 * count, depth))],
        out_shape=[
            jax.ShapeDtypeStruct((4, 16 * count, width), BF),
            jax.ShapeDtypeStruct((4, 16 * count, width), BF),
            jax.ShapeDtypeStruct((4, 2 * count, depth), F32),
        ],
        scratch_shapes=[pltpu.VMEM((8, 4, 4 * count, depth), BF)],
        compiler_params=pltpu.CompilerParams(vmem_limit_bytes=(10 + 2 * count) * 2**20),
        cost_estimate=cost(count, width, depth),
    )(pos, near_pair, wide_pair, weight)


def cost(count, width, depth):
    rows = 128 * count
    return pl.CostEstimate(
        flops=2 * rows * width * depth,
        bytes_accessed=2 * (width * depth + rows * (width + depth)),
        transcendentals=0,
    )


def feature_kernel(chunk, pos, near_same, wide_same, near_other, wide_other, weight, keep, send, lhs, result):
    x, y, z, c = pos[0], pos[1], pos[2], pos[3]

    @pl.when(pl.program_id(0) == 0)
    def _():
        for c_rel, (near_pair, wide_pair) in enumerate(((near_same, wide_same), (near_other, wide_other))):
            core = jnp.bitwise_xor(c, c_rel)
            for j, flip in enumerate(ring_order(chunk, core)):
                ref = near_pair if j < 2 else wide_pair
                lhs[2 * jnp.bitwise_xor(y, flip) + core] = ref[j % 2]

    rows = lhs[...].reshape(-1, lhs.shape[-1])
    result[...] = nt_dot(rows, weight[...]).reshape(result.shape)
    for x_rel, x_flip in enumerate(ring_order(chunk, c)):
        to = jnp.bitwise_xor(x, x_flip)
        out = keep if x_rel < 2 else send
        for z_rel, z_flip in enumerate((0, 2, 1, 3)):
            rows = result[2 * jnp.bitwise_xor(z, z_flip) + to // 2, :, lax.rem(to, 2)]
            out[x_rel % 2, z_rel] = rows.reshape(out.shape[2], -1).astype(BF)


def feature_product(chunk, pos, pairs, weight):
    width, depth = weight.shape
    tile = min(256, width)
    count = COUNTS[chunk]
    out_block = pl.BlockSpec((2, 4, 8 * count, tile), lambda i: (0, 0, 0, i))
    return pl.pallas_call(
        functools.partial(feature_kernel, chunk),
        grid=(width // tile,),
        in_specs=[SMEM] + [full(pair.shape) for pair in pairs] + [pl.BlockSpec((tile, depth), lambda i: (i, 0))],
        out_specs=[out_block, out_block],
        out_shape=[jax.ShapeDtypeStruct((2, 4, 8 * count, width), BF)] * 2,
        scratch_shapes=[
            pltpu.VMEM((8, 16 * count, depth), BF),
            pltpu.VMEM((8, 4, 2, 2 * count, tile), F32),
        ],
        compiler_params=pltpu.CompilerParams(vmem_limit_bytes=(10 + 3 * count) * 2**20),
        cost_estimate=cost(count, width, depth),
    )(pos, *pairs, weight)


def add(*terms):
    return functools.reduce(jnp.add, [term.astype(F32) for term in terms])


def sort_flips(pieces, at):
    a0, a1, a2, a3 = pieces
    odd, high = at % 2 == 1, at >= 2
    a0, a1 = jnp.where(odd, a1, a0), jnp.where(odd, a0, a1)
    a2, a3 = jnp.where(odd, a3, a2), jnp.where(odd, a2, a3)
    a0, a2 = jnp.where(high, a2, a0), jnp.where(high, a0, a2)
    a1, a3 = jnp.where(high, a3, a1), jnp.where(high, a1, a3)
    return a0, a1, a2, a3


def own_features(rows, y, c):
    depth = rows.shape[1] // 8
    parts = [jnp.stack([rows[:, (2 * i + core) * depth :][:, :depth] for i in range(4)]) for core in range(2)]
    low = c == 0
    mine = jnp.where(low, parts[0], parts[1])
    other = move_core(jnp.where(low, parts[1], parts[0]))
    both = jnp.stack([jnp.where(low, mine, other), jnp.where(low, other, mine)], axis=1)

    def block(flip):
        return lax.dynamic_index_in_dim(both, y ^ flip, 0, keepdims=False)

    pieces = [block(0)] + [move_y(block(flip), flip) for flip in (1, 2, 3)]
    return jnp.concatenate(sort_flips(pieces, y)).transpose(1, 0, 2)


def gather_rows(chunk, part, z):
    a3 = move_mirror(part)
    a1 = move_z(a3, 2)
    a2, a0 = move_z(jnp.stack([a3, a1]), 1)
    own = jnp.concatenate(sort_flips((a0, a1, a2, a3), z)).transpose(1, 0, 2)
    return gather_ring(chunk, own, "x")


def gather_ring(chunk, block, axis):
    first, second = flips(chunk)
    pair = jnp.stack([block, move_ring(block, axis, first)])
    return pair, move_ring(pair, axis, second)


def reduce_hidden(chunk, keep, send):
    second, first = flips(chunk)
    other = move_core(send)
    far = move_ring(add(keep[2:], other[2:]).astype(BF), "y", first)
    last = move_ring(add(keep[1], other[1], far[1]).astype(BF), "y", second)
    return add(keep[0], other[0], far[0], last)


def reduce_features(chunk, keep, send):
    second, first = flips(chunk)
    far = move_ring(send, "x", first)
    last = move_ring(add(keep[1], far[1]).astype(BF), "x", second)
    total = add(keep[0], far[0], last)
    far = move_z(total[2:].astype(BF), 1)
    last = move_z(add(total[1], far[1]).astype(BF), 2)
    return add(total[0], far[0], last)


def sum_over_dp(array):
    array = array + move_core(array)
    return array + move_y(array, 1) + move_y(array, 2) + move_y(array, 3)


def per_device(
    loss_sensitivity_outgoing,
    expansion_factor,
    contraction_factor,
    intermediate_affine_values,
    centered_unscaled_entry,
    inverse_spread_per_position,
    layernorm_multiplier,
):
    x, y, z, c = (lax.axis_index(name) for name in ("x", "y", "z", "core"))
    pos = jnp.stack([x, y, z, c]).astype(jnp.int32)
    model = 8 * expansion_factor.shape[1]
    rows = own_features(loss_sensitivity_outgoing[0], y, c)
    slope = slope_rows(intermediate_affine_values[0])

    def by_chunk(array):
        array = array.reshape(2, 4, 12, *array.shape[1:])
        parts = [array[:, :, start : start + count] for start, count in zip(STARTS, COUNTS)]
        return [part.swapaxes(0, 1).reshape(-1, *part.shape[3:]) for part in parts]

    entry = by_chunk(centered_unscaled_entry[0].astype(F32))
    spread = by_chunk(inverse_spread_per_position[0])
    gain = layernorm_multiplier[0]
    rows, slope = lax.optimization_barrier((rows, slope))

    mine, scaled = [], []
    for k, (start, count) in enumerate(zip(STARTS, COUNTS)):
        gathered = gather_rows(k, rows[start : start + count], z)
        keep, send, own_rows = hidden_product(k, pos, *gathered, contraction_factor[0])
        block = (reduce_hidden(k, keep, send) * slope[k]).astype(BF)
        near_pair, wide_pair = gather_ring(k, block, "y")
        pairs = (near_pair, wide_pair, move_core(near_pair), move_core(wide_pair))
        keep, send = feature_product(k, pos, pairs, expansion_factor[0])
        mine.append(own_rows.reshape(8 * count, -1))
        scaled.append(gain * reduce_features(k, keep, send))
    sums = [jnp.stack([jnp.sum(part, axis=1), jnp.sum(part * known, axis=1)]) for part, known in zip(scaled, entry)]
    sums = sum_over_dp(jnp.concatenate(sums, axis=1)) / model
    parts = []
    for k, (start, count) in enumerate(zip(STARTS, COUNTS)):
        first, second = sums[:, 8 * start : 8 * (start + count), None]
        result = mine[k] + spread[k][:, None] * (scaled[k] - first - entry[k] * second)
        parts.append(result.astype(BF).reshape(4, 2, count, -1).swapaxes(0, 1))
    return jnp.concatenate(parts, axis=2).reshape(1, 96, -1)


def solution(mesh):
    split = Mesh(mesh.devices.reshape(2, 4, 2, 4, 4), ("section", "y", "core", "z", "x"))
    dp, mp = ("y", "core"), ("z", "x")
    in_specs = (
        P("section", dp + mp, None),
        P("section", dp, mp),
        P("section", mp, dp),
        P("section", dp, mp),
        P("section", mp, dp),
        P("section", mp),
        P("section", dp),
    )
    out_specs = P("section", mp, dp)
    return jax.shard_map(per_device, mesh=split, in_specs=in_specs, out_specs=out_specs, check_vma=False)
```

```python
import functools
import math

import jax
import jax.numpy as jnp
from jax import lax
from jax.experimental import pallas as pl
from jax.experimental.pallas import tpu as pltpu
from jax.sharding import Mesh, PartitionSpec as P

BF = jnp.bfloat16
F32 = jnp.float32
CHUNKS = 3
ROWS = 12 // CHUNKS


def near(core):
    return 1 + 2 * core


def wide(core):
    return 3 - 2 * core


def move_ring(array, axis, flip):
    pairs = [(c, i, c, i ^ flip(c)) for c in range(2) for i in range(4)]
    if axis == "y":
        return lax.ppermute(array, ("y", "core"), [(2 * i + c, 2 * j + d) for c, i, d, j in pairs])
    return lax.ppermute(array, ("core", axis), [(4 * c + i, 4 * d + j) for c, i, d, j in pairs])


def move_y(array, flip):
    return lax.ppermute(array, "y", [(y, y ^ flip) for y in range(4)])


def move_z(array, flip):
    return lax.ppermute(array, "z", [(z, z ^ flip) for z in range(4)])


def move_mirror(array):
    return lax.ppermute(array, ("section", "z"), [(i, 7 - i) for i in range(8)])


def move_core(array):
    return lax.ppermute(array, "core", [(0, 1), (1, 0)])


def flips(chunk):
    return (near, wide) if chunk % 2 == 0 else (wide, near)


def ring_order(chunk, core):
    first, second = flips(chunk)
    return 0, first(core), second(core), 2


def gelu_slope(u):
    c = math.sqrt(2.0 / math.pi)
    t = jnp.tanh(c * (u + 0.044715 * u * u * u))
    return 0.5 * (1.0 + t) + 0.5 * u * (1.0 - t * t) * c * (1.0 + 3.0 * 0.044715 * u * u)


def nt_dot(left, right):
    return lax.dot_general(left, right, (((1,), (1,)), ((), ())), preferred_element_type=F32)


def full(shape):
    return pl.BlockSpec(shape, lambda i: (0,) * len(shape))


SMEM = pl.BlockSpec(memory_space=pltpu.SMEM)


def slope_kernel(u, *outs):
    values = gelu_slope(u[...].astype(F32))
    for k in range(CHUNKS):
        pieces = []
        for x in range(4):
            for z in range(4):
                start = (4 * z + x) * 12 + ROWS * k
                pieces.append(values[start : start + ROWS])
        outs[k][...] = jnp.concatenate(pieces, axis=0)


def slope_rows(u):
    rows, width = u.shape
    tile = min(512, width)
    return pl.pallas_call(
        slope_kernel,
        grid=(width // tile,),
        in_specs=[pl.BlockSpec((rows, tile), lambda i: (0, i))],
        out_specs=[pl.BlockSpec((rows // CHUNKS, tile), lambda i: (0, i))] * CHUNKS,
        out_shape=[jax.ShapeDtypeStruct((rows // CHUNKS, width), F32)] * CHUNKS,
        compiler_params=pltpu.CompilerParams(vmem_limit_bytes=16 * 2**20),
        cost_estimate=pl.CostEstimate(flops=20 * rows * width, bytes_accessed=6 * rows * width, transcendentals=rows * width),
    )(u)


def hidden_kernel(chunk, pos, near_pair, wide_pair, weight, keep, send, mine, lhs):
    x, y, z, c = pos[0], pos[1], pos[2], pos[3]

    @pl.when(pl.program_id(0) == 0)
    def _():
        for c_rel in range(2):
            core = jnp.bitwise_xor(c, c_rel)
            for j, flip in enumerate(ring_order(chunk, core)):
                source = 2 * jnp.bitwise_xor(y, flip) + core
                for x_rel, x_flip in enumerate(ring_order(chunk, c)):
                    ref = near_pair if x_rel < 2 else wide_pair
                    lhs[4 * c_rel + j, jnp.bitwise_xor(x, x_flip)] = ref[x_rel % 2, source]
        source = 2 * z + x // 2
        for x_rel, x_flip in enumerate(ring_order(chunk, c)):
            ref = near_pair if x_rel < 2 else wide_pair
            rows = ref[x_rel % 2, source].astype(F32)
            picked = jnp.where(lax.rem(x, 2) == 0, rows[:8], rows[8:])
            mine[jnp.bitwise_xor(x, x_flip)] = picked

    rows = lhs[...].reshape(512, -1)
    product = nt_dot(rows, weight[...]).astype(BF)
    keep[...] = product[:256].reshape(keep.shape)
    send[...] = product[256:].reshape(send.shape)


def hidden_product(chunk, pos, near_pair, wide_pair, weight):
    width, depth = weight.shape
    tile = min(512, width)
    out_block = pl.BlockSpec((4, 64, tile), lambda i: (0, 0, i))
    return pl.pallas_call(
        functools.partial(hidden_kernel, chunk),
        grid=(width // tile,),
        in_specs=[
            SMEM,
            full(near_pair.shape),
            full(wide_pair.shape),
            pl.BlockSpec((tile, depth), lambda i: (i, 0)),
        ],
        out_specs=[out_block, out_block, full((4, 8, depth))],
        out_shape=[
            jax.ShapeDtypeStruct((4, 64, width), BF),
            jax.ShapeDtypeStruct((4, 64, width), BF),
            jax.ShapeDtypeStruct((4, 8, depth), F32),
        ],
        scratch_shapes=[pltpu.VMEM((8, 4, 16, depth), BF)],
        compiler_params=pltpu.CompilerParams(vmem_limit_bytes=16 * 2**20),
        cost_estimate=pl.CostEstimate(
            flops=2 * 512 * width * depth, bytes_accessed=2 * (width * depth + 512 * (width + depth)), transcendentals=0
        ),
    )(pos, near_pair, wide_pair, weight)


def feature_kernel(chunk, pos, near_same, wide_same, near_other, wide_other, weight, keep, send, lhs, result):
    x, y, z, c = pos[0], pos[1], pos[2], pos[3]

    @pl.when(pl.program_id(0) == 0)
    def _():
        for c_rel, (near_pair, wide_pair) in enumerate(((near_same, wide_same), (near_other, wide_other))):
            core = jnp.bitwise_xor(c, c_rel)
            for j, flip in enumerate(ring_order(chunk, core)):
                ref = near_pair if j < 2 else wide_pair
                lhs[2 * jnp.bitwise_xor(y, flip) + core] = ref[j % 2]

    rows = lhs[...].reshape(512, -1)
    result[...] = nt_dot(rows, weight[...]).reshape(result.shape)
    for x_rel, x_flip in enumerate(ring_order(chunk, c)):
        to = jnp.bitwise_xor(x, x_flip)
        out = keep if x_rel < 2 else send
        for z_rel, z_flip in enumerate((0, 2, 1, 3)):
            rows = result[2 * jnp.bitwise_xor(z, z_flip) + to // 2, :, lax.rem(to, 2)]
            out[x_rel % 2, z_rel] = rows.reshape(32, -1).astype(BF)


def feature_product(chunk, pos, pairs, weight):
    width, depth = weight.shape
    tile = min(256, width)
    out_block = pl.BlockSpec((2, 4, 32, tile), lambda i: (0, 0, 0, i))
    return pl.pallas_call(
        functools.partial(feature_kernel, chunk),
        grid=(width // tile,),
        in_specs=[SMEM] + [full(pair.shape) for pair in pairs] + [pl.BlockSpec((tile, depth), lambda i: (i, 0))],
        out_specs=[out_block, out_block],
        out_shape=[jax.ShapeDtypeStruct((2, 4, 32, width), BF)] * 2,
        scratch_shapes=[pltpu.VMEM((8, 64, depth), BF), pltpu.VMEM((8, 4, 2, 8, tile), F32)],
        compiler_params=pltpu.CompilerParams(vmem_limit_bytes=20 * 2**20),
        cost_estimate=pl.CostEstimate(
            flops=2 * 512 * width * depth, bytes_accessed=2 * (width * depth + 512 * (width + depth)), transcendentals=0
        ),
    )(pos, *pairs, weight)


def add(*terms):
    return functools.reduce(jnp.add, [term.astype(F32) for term in terms])


def sort_flips(pieces, at):
    a0, a1, a2, a3 = pieces
    odd, high = at % 2 == 1, at >= 2
    a0, a1 = jnp.where(odd, a1, a0), jnp.where(odd, a0, a1)
    a2, a3 = jnp.where(odd, a3, a2), jnp.where(odd, a2, a3)
    a0, a2 = jnp.where(high, a2, a0), jnp.where(high, a0, a2)
    a1, a3 = jnp.where(high, a3, a1), jnp.where(high, a1, a3)
    return a0, a1, a2, a3


def own_features(rows, y, c):
    depth = rows.shape[1] // 8
    parts = [jnp.stack([rows[:, (2 * i + core) * depth :][:, :depth] for i in range(4)]) for core in range(2)]
    low = c == 0
    mine = jnp.where(low, parts[0], parts[1])
    other = move_core(jnp.where(low, parts[1], parts[0]))
    both = jnp.stack([jnp.where(low, mine, other), jnp.where(low, other, mine)], axis=1)

    def block(flip):
        return lax.dynamic_index_in_dim(both, y ^ flip, 0, keepdims=False)

    pieces = [block(0)] + [move_y(block(flip), flip) for flip in (1, 2, 3)]
    return jnp.concatenate(sort_flips(pieces, y)).transpose(1, 0, 2)


def in_step(arrays):
    return lax.optimization_barrier(list(arrays))


def gather_rows(rows, z):
    chunks = range(CHUNKS)
    a3 = in_step(move_mirror(rows[ROWS * k : ROWS * (k + 1)]) for k in chunks)
    a1 = in_step(move_z(a3[k], 2) for k in chunks)
    moved = in_step(move_z(jnp.stack([a3[k], a1[k]]), 1) for k in chunks)
    own = []
    for k in chunks:
        pieces = sort_flips((moved[k][1], a1[k], moved[k][0], a3[k]), z)
        own.append(jnp.concatenate(pieces).transpose(1, 0, 2))
    moved = in_step(move_ring(own[k], "x", flips(k)[0]) for k in chunks)
    pairs = [jnp.stack([own[k], moved[k]]) for k in chunks]
    return [(pairs[k], move_ring(pairs[k], "x", flips(k)[1])) for k in chunks]


def gather_ring(chunk, block, axis):
    first, second = flips(chunk)
    pair = jnp.stack([block, move_ring(block, axis, first)])
    return pair, move_ring(pair, axis, second)


def reduce_hidden(chunk, keep, send):
    second, first = flips(chunk)
    other = move_core(send)
    far = move_ring(add(keep[2:], other[2:]).astype(BF), "y", first)
    last = move_ring(add(keep[1], other[1], far[1]).astype(BF), "y", second)
    return add(keep[0], other[0], far[0], last)


def reduce_features(chunk, keep, send):
    second, first = flips(chunk)
    far = move_ring(send, "x", first)
    last = move_ring(add(keep[1], far[1]).astype(BF), "x", second)
    total = add(keep[0], far[0], last)
    far = move_z(total[2:].astype(BF), 1)
    last = move_z(add(total[1], far[1]).astype(BF), 2)
    return add(total[0], far[0], last)


def sum_over_dp(array):
    array = array + move_core(array)
    return array + move_y(array, 1) + move_y(array, 2) + move_y(array, 3)


def per_device(
    loss_sensitivity_outgoing,
    expansion_factor,
    contraction_factor,
    intermediate_affine_values,
    centered_unscaled_entry,
    inverse_spread_per_position,
    layernorm_multiplier,
):
    x, y, z, c = (lax.axis_index(name) for name in ("x", "y", "z", "core"))
    pos = jnp.stack([x, y, z, c]).astype(jnp.int32)
    model = 8 * expansion_factor.shape[1]
    rows = own_features(loss_sensitivity_outgoing[0], y, c)
    slope = slope_rows(intermediate_affine_values[0])

    def by_chunk(array):
        rest = array.shape[1:]
        array = array.reshape(2, 4, CHUNKS, ROWS, *rest)
        array = array.transpose(2, 1, 0, 3, *range(4, array.ndim))
        return array.reshape(CHUNKS, 32, *rest)

    entry = by_chunk(centered_unscaled_entry[0]).astype(F32)
    spread = by_chunk(inverse_spread_per_position[0])
    gain = layernorm_multiplier[0]

    rows, slope = lax.optimization_barrier((rows, slope))
    gathered = gather_rows(rows, z)
    mine, scaled = [], []
    for k in range(CHUNKS):
        keep, send, own_rows = hidden_product(k, pos, *gathered[k], contraction_factor[0])
        block = (reduce_hidden(k, keep, send) * slope[k]).astype(BF)
        near_pair, wide_pair = gather_ring(k, block, "y")
        pairs = (near_pair, wide_pair, move_core(near_pair), move_core(wide_pair))
        keep, send = feature_product(k, pos, pairs, expansion_factor[0])
        mine.append(own_rows.reshape(32, -1))
        scaled.append(gain * reduce_features(k, keep, send))
    scaled = jnp.stack(scaled)
    upstream = jnp.stack(mine)
    sums = sum_over_dp(jnp.stack([jnp.sum(scaled, axis=2), jnp.sum(scaled * entry, axis=2)]))
    result = upstream + spread[:, :, None] * (
        scaled - sums[0][:, :, None] / model - entry * sums[1][:, :, None] / model
    )
    result = result.reshape(CHUNKS, 4, 2, ROWS, -1).transpose(2, 1, 0, 3, 4)
    return result.reshape(1, 96, -1).astype(BF)


def solution(mesh):
    split = Mesh(mesh.devices.reshape(2, 4, 2, 4, 4), ("section", "y", "core", "z", "x"))
    dp, mp = ("y", "core"), ("z", "x")
    in_specs = (
        P("section", dp + mp, None),
        P("section", dp, mp),
        P("section", mp, dp),
        P("section", dp, mp),
        P("section", mp, dp),
        P("section", mp),
        P("section", dp),
    )
    out_specs = P("section", mp, dp)
    return jax.shard_map(per_device, mesh=split, in_specs=in_specs, out_specs=out_specs, check_vma=False)
```

```python
import functools
import math

import jax
import jax.numpy as jnp
from jax import lax
from jax.experimental import pallas as pl
from jax.experimental.pallas import tpu as pltpu
from jax.sharding import Mesh, PartitionSpec as P

BF = jnp.bfloat16
F32 = jnp.float32
CHUNKS = 3
ROWS = 12 // CHUNKS


def near(core):
    return 1 + 2 * core


def wide(core):
    return 3 - 2 * core


def move_ring(array, axis, flip):
    pairs = [(c, i, c, i ^ flip(c)) for c in range(2) for i in range(4)]
    if axis == "y":
        return lax.ppermute(array, ("y", "core"), [(2 * i + c, 2 * j + d) for c, i, d, j in pairs])
    return lax.ppermute(array, ("core", axis), [(4 * c + i, 4 * d + j) for c, i, d, j in pairs])


def move_y(array, flip):
    return lax.ppermute(array, "y", [(y, y ^ flip) for y in range(4)])


def move_z(array, flip):
    return lax.ppermute(array, "z", [(z, z ^ flip) for z in range(4)])


def move_mirror(array):
    return lax.ppermute(array, ("section", "z"), [(i, 7 - i) for i in range(8)])


def move_core(array):
    return lax.ppermute(array, "core", [(0, 1), (1, 0)])


def flips(chunk):
    return (near, wide) if chunk % 2 == 0 else (wide, near)


def ring_order(chunk, core):
    first, second = flips(chunk)
    return 0, first(core), second(core), 2


def gelu_slope(u):
    c = math.sqrt(2.0 / math.pi)
    t = jnp.tanh(c * (u + 0.044715 * u * u * u))
    return 0.5 * (1.0 + t) + 0.5 * u * (1.0 - t * t) * c * (1.0 + 3.0 * 0.044715 * u * u)


def nt_dot(left, right):
    return lax.dot_general(left, right, (((1,), (1,)), ((), ())), preferred_element_type=F32)


def full(shape):
    return pl.BlockSpec(shape, lambda i: (0,) * len(shape))


SMEM = pl.BlockSpec(memory_space=pltpu.SMEM)


def slope_kernel(u, *outs):
    values = gelu_slope(u[...].astype(F32))
    for k in range(CHUNKS):
        pieces = []
        for x in range(4):
            for z in range(4):
                start = (4 * z + x) * 12 + ROWS * k
                pieces.append(values[start : start + ROWS])
        outs[k][...] = jnp.concatenate(pieces, axis=0)


def slope_rows(u):
    rows, width = u.shape
    tile = min(512, width)
    return pl.pallas_call(
        slope_kernel,
        grid=(width // tile,),
        in_specs=[pl.BlockSpec((rows, tile), lambda i: (0, i))],
        out_specs=[pl.BlockSpec((rows // CHUNKS, tile), lambda i: (0, i))] * CHUNKS,
        out_shape=[jax.ShapeDtypeStruct((rows // CHUNKS, width), F32)] * CHUNKS,
        compiler_params=pltpu.CompilerParams(vmem_limit_bytes=16 * 2**20),
        cost_estimate=pl.CostEstimate(flops=20 * rows * width, bytes_accessed=6 * rows * width, transcendentals=rows * width),
    )(u)


def hidden_kernel(chunk, pos, near_pair, wide_pair, weight, keep, send, mine, lhs):
    x, y, z, c = pos[0], pos[1], pos[2], pos[3]

    @pl.when(pl.program_id(0) == 0)
    def _():
        for c_rel in range(2):
            core = jnp.bitwise_xor(c, c_rel)
            for j, flip in enumerate(ring_order(chunk, core)):
                source = 2 * jnp.bitwise_xor(y, flip) + core
                for x_rel, x_flip in enumerate(ring_order(chunk, c)):
                    ref = near_pair if x_rel < 2 else wide_pair
                    lhs[4 * c_rel + j, jnp.bitwise_xor(x, x_flip)] = ref[x_rel % 2, source]
        source = 2 * z + x // 2
        for x_rel, x_flip in enumerate(ring_order(chunk, c)):
            ref = near_pair if x_rel < 2 else wide_pair
            rows = ref[x_rel % 2, source].astype(F32)
            picked = jnp.where(lax.rem(x, 2) == 0, rows[:8], rows[8:])
            mine[jnp.bitwise_xor(x, x_flip)] = picked

    rows = lhs[...].reshape(512, -1)
    product = nt_dot(rows, weight[...]).astype(BF)
    keep[...] = product[:256].reshape(keep.shape)
    send[...] = product[256:].reshape(send.shape)


def hidden_product(chunk, pos, near_pair, wide_pair, weight):
    width, depth = weight.shape
    tile = min(256, width)
    out_block = pl.BlockSpec((4, 64, tile), lambda i: (0, 0, i))
    return pl.pallas_call(
        functools.partial(hidden_kernel, chunk),
        grid=(width // tile,),
        in_specs=[
            SMEM,
            full(near_pair.shape),
            full(wide_pair.shape),
            pl.BlockSpec((tile, depth), lambda i: (i, 0)),
        ],
        out_specs=[out_block, out_block, full((4, 8, depth))],
        out_shape=[
            jax.ShapeDtypeStruct((4, 64, width), BF),
            jax.ShapeDtypeStruct((4, 64, width), BF),
            jax.ShapeDtypeStruct((4, 8, depth), F32),
        ],
        scratch_shapes=[pltpu.VMEM((8, 4, 16, depth), BF)],
        compiler_params=pltpu.CompilerParams(vmem_limit_bytes=16 * 2**20),
        cost_estimate=pl.CostEstimate(
            flops=2 * 512 * width * depth, bytes_accessed=2 * (width * depth + 512 * (width + depth)), transcendentals=0
        ),
    )(pos, near_pair, wide_pair, weight)


def feature_kernel(chunk, pos, near_same, wide_same, other, weight, keep, send, lhs, result):
    x, y, z, c = pos[0], pos[1], pos[2], pos[3]

    @pl.when(pl.program_id(0) == 0)
    def _():
        for j, flip in enumerate(ring_order(chunk, c)):
            lhs[2 * jnp.bitwise_xor(y, flip) + c] = (near_same if j < 2 else wide_same)[j % 2]
        for j, flip in enumerate(ring_order(chunk, 1 - c)):
            lhs[2 * jnp.bitwise_xor(y, flip) + 1 - c] = other[j]

    rows = lhs[...].reshape(512, -1)
    result[...] = nt_dot(rows, weight[...]).reshape(result.shape)
    for x_rel, x_flip in enumerate(ring_order(chunk, c)):
        to = jnp.bitwise_xor(x, x_flip)
        out = keep if x_rel < 2 else send
        for z_rel, z_flip in enumerate((0, 2, 1, 3)):
            rows = result[2 * jnp.bitwise_xor(z, z_flip) + to // 2, :, lax.rem(to, 2)]
            out[x_rel % 2, z_rel] = rows.reshape(32, -1).astype(BF)


def feature_product(chunk, pos, pairs, weight):
    width, depth = weight.shape
    tile = min(256, width)
    out_block = pl.BlockSpec((2, 4, 32, tile), lambda i: (0, 0, 0, i))
    return pl.pallas_call(
        functools.partial(feature_kernel, chunk),
        grid=(width // tile,),
        in_specs=[SMEM] + [full(pair.shape) for pair in pairs] + [pl.BlockSpec((tile, depth), lambda i: (i, 0))],
        out_specs=[out_block, out_block],
        out_shape=[jax.ShapeDtypeStruct((2, 4, 32, width), BF)] * 2,
        scratch_shapes=[pltpu.VMEM((8, 64, depth), BF), pltpu.VMEM((8, 4, 2, 8, tile), F32)],
        compiler_params=pltpu.CompilerParams(vmem_limit_bytes=20 * 2**20),
        cost_estimate=pl.CostEstimate(
            flops=2 * 512 * width * depth, bytes_accessed=2 * (width * depth + 512 * (width + depth)), transcendentals=0
        ),
    )(pos, *pairs, weight)


def add(*terms):
    return functools.reduce(jnp.add, [term.astype(F32) for term in terms])


def sort_flips(pieces, at):
    a0, a1, a2, a3 = pieces
    odd, high = at % 2 == 1, at >= 2
    a0, a1 = jnp.where(odd, a1, a0), jnp.where(odd, a0, a1)
    a2, a3 = jnp.where(odd, a3, a2), jnp.where(odd, a2, a3)
    a0, a2 = jnp.where(high, a2, a0), jnp.where(high, a0, a2)
    a1, a3 = jnp.where(high, a3, a1), jnp.where(high, a1, a3)
    return a0, a1, a2, a3


def own_features(rows, y, c):
    depth = rows.shape[1] // 8
    parts = [jnp.stack([rows[:, (2 * i + core) * depth :][:, :depth] for i in range(4)]) for core in range(2)]
    low = c == 0
    mine = jnp.where(low, parts[0], parts[1])
    other = move_core(jnp.where(low, parts[1], parts[0]))
    both = jnp.stack([jnp.where(low, mine, other), jnp.where(low, other, mine)], axis=1)

    def blocks(*flips_y):
        return jnp.stack([lax.dynamic_index_in_dim(both, y ^ flip, 0, keepdims=False) for flip in flips_y])

    moved = move_y(blocks(1, 2), 1)
    kept = blocks(0, 3)
    far = move_y(jnp.stack([kept[1], moved[1]]), 3)
    return jnp.concatenate(sort_flips((kept[0], moved[0], far[1], far[0]), y)).transpose(1, 0, 2)


def gather_z(rows, z):
    a3 = move_mirror(rows)
    a1 = move_z(a3, 2)
    a2, a0 = move_z(jnp.stack([a3, a1]), 1)
    pieces = sort_flips((a0, a1, a2, a3), z)
    starts = range(0, rows.shape[0], ROWS)
    return [jnp.concatenate([piece[at : at + ROWS] for piece in pieces]).transpose(1, 0, 2) for at in starts]


def gather_ring(chunk, block, axis):
    first, second = flips(chunk)
    pair = jnp.stack([block, move_ring(block, axis, first)])
    return pair, move_ring(pair, axis, second)


def reduce_hidden(chunk, keep, send):
    second, first = flips(chunk)
    other = move_core(send)
    far = move_ring(add(keep[2:], other[2:]).astype(BF), "y", first)
    last = move_ring(add(keep[1], other[1], far[1]).astype(BF), "y", second)
    return add(keep[0], other[0], far[0], last)


def reduce_x(chunk, keep, send):
    second, first = flips(chunk)
    far = move_ring(send, "x", first)
    last = move_ring(add(keep[1], far[1]).astype(BF), "x", second)
    return add(keep[0], far[0], last)


def reduce_z(totals):
    total = jnp.stack(totals, axis=1)
    far = move_z(total[2:].astype(BF), 1)
    last = move_z(add(total[1], far[1]).astype(BF), 2)
    return list(add(total[0], far[0], last))


def sum_over_dp(array):
    array = array + move_core(array)
    array = array + move_y(array, 1)
    return array + move_y(array, 3)


def per_device(
    loss_sensitivity_outgoing,
    expansion_factor,
    contraction_factor,
    intermediate_affine_values,
    centered_unscaled_entry,
    inverse_spread_per_position,
    layernorm_multiplier,
):
    x, y, z, c = (lax.axis_index(name) for name in ("x", "y", "z", "core"))
    pos = jnp.stack([x, y, z, c]).astype(jnp.int32)
    model = 8 * expansion_factor.shape[1]
    rows = own_features(loss_sensitivity_outgoing[0], y, c)
    slope = slope_rows(intermediate_affine_values[0])

    def by_chunk(array):
        rest = array.shape[1:]
        array = array.reshape(2, 4, CHUNKS, ROWS, *rest)
        array = array.transpose(2, 1, 0, 3, *range(4, array.ndim))
        return array.reshape(CHUNKS, 32, *rest)

    entry = by_chunk(centered_unscaled_entry[0]).astype(F32)
    spread = by_chunk(inverse_spread_per_position[0])
    gain = layernorm_multiplier[0]

    rows, slope = lax.optimization_barrier((rows, slope))
    parts = gather_z(rows[:ROWS], z) + gather_z(rows[ROWS:], z)
    mine, totals = [], []
    for k in range(CHUNKS):
        keep, send, own_rows = hidden_product(k, pos, *gather_ring(k, parts[k], "x"), contraction_factor[0])
        block = (reduce_hidden(k, keep, send) * slope[k]).astype(BF)
        near_pair, wide_pair = gather_ring(k, block, "y")
        other = move_core(jnp.concatenate([near_pair, wide_pair]))
        keep, send = feature_product(k, pos, (near_pair, wide_pair, other), expansion_factor[0])
        mine.append(own_rows.reshape(32, -1))
        totals.append(reduce_x(k, keep, send))
    scaled = [gain * total for total in reduce_z(totals[:2]) + reduce_z(totals[2:])]
    scaled = jnp.stack(scaled)
    upstream = jnp.stack(mine)
    sums = sum_over_dp(jnp.stack([jnp.sum(scaled, axis=2), jnp.sum(scaled * entry, axis=2)]))
    result = upstream + spread[:, :, None] * (
        scaled - sums[0][:, :, None] / model - entry * sums[1][:, :, None] / model
    )
    result = result.reshape(CHUNKS, 4, 2, ROWS, -1).transpose(2, 1, 0, 3, 4)
    return result.reshape(1, 96, -1).astype(BF)


def solution(mesh):
    split = Mesh(mesh.devices.reshape(2, 4, 2, 4, 4), ("section", "y", "core", "z", "x"))
    dp, mp = ("y", "core"), ("z", "x")
    in_specs = (
        P("section", dp + mp, None),
        P("section", dp, mp),
        P("section", mp, dp),
        P("section", dp, mp),
        P("section", mp, dp),
        P("section", mp),
        P("section", dp),
    )
    out_specs = P("section", mp, dp)
    return jax.shard_map(per_device, mesh=split, in_specs=in_specs, out_specs=out_specs, check_vma=False)
```

```python
import functools
import math

import jax
import jax.numpy as jnp
from jax import lax
from jax.experimental import pallas as pl
from jax.experimental.pallas import tpu as pltpu
from jax.sharding import Mesh, PartitionSpec as P

BF = jnp.bfloat16
F32 = jnp.float32
CHUNKS = 3
ROWS = 12 // CHUNKS


def near(core):
    return 1 + 2 * core


def wide(core):
    return 3 - 2 * core


def move_ring(array, axis, flip):
    pairs = [(c, i, c, i ^ flip(c)) for c in range(2) for i in range(4)]
    if axis == "y":
        return lax.ppermute(array, ("y", "core"), [(2 * i + c, 2 * j + d) for c, i, d, j in pairs])
    return lax.ppermute(array, ("core", axis), [(4 * c + i, 4 * d + j) for c, i, d, j in pairs])


def move_y(array, flip):
    return lax.ppermute(array, "y", [(y, y ^ flip) for y in range(4)])


def move_z(array, flip):
    return lax.ppermute(array, "z", [(z, z ^ flip) for z in range(4)])


def move_mirror(array):
    return lax.ppermute(array, ("section", "z"), [(i, 7 - i) for i in range(8)])


def move_core(array):
    return lax.ppermute(array, "core", [(0, 1), (1, 0)])


def flips(chunk):
    return (near, wide) if chunk % 2 == 0 else (wide, near)


def ring_order(chunk, core):
    first, second = flips(chunk)
    return 0, first(core), second(core), 2


def gelu_slope(u):
    c = math.sqrt(2.0 / math.pi)
    t = jnp.tanh(c * (u + 0.044715 * u * u * u))
    return 0.5 * (1.0 + t) + 0.5 * u * (1.0 - t * t) * c * (1.0 + 3.0 * 0.044715 * u * u)


def nt_dot(left, right):
    return lax.dot_general(left, right, (((1,), (1,)), ((), ())), preferred_element_type=F32)


def full(shape):
    return pl.BlockSpec(shape, lambda i: (0,) * len(shape))


SMEM = pl.BlockSpec(memory_space=pltpu.SMEM)


def slope_kernel(u, *outs):
    values = gelu_slope(u[...].astype(F32))
    for k in range(CHUNKS):
        pieces = []
        for x in range(4):
            for z in range(4):
                start = (4 * z + x) * 12 + ROWS * k
                pieces.append(values[start : start + ROWS])
        outs[k][...] = jnp.concatenate(pieces, axis=0)


def slope_rows(u):
    rows, width = u.shape
    tile = min(256, width)
    return pl.pallas_call(
        slope_kernel,
        grid=(width // tile,),
        in_specs=[pl.BlockSpec((rows, tile), lambda i: (0, i))],
        out_specs=[pl.BlockSpec((rows // CHUNKS, tile), lambda i: (0, i))] * CHUNKS,
        out_shape=[jax.ShapeDtypeStruct((rows // CHUNKS, width), F32)] * CHUNKS,
        compiler_params=pltpu.CompilerParams(vmem_limit_bytes=16 * 2**20),
        cost_estimate=pl.CostEstimate(flops=20 * rows * width, bytes_accessed=6 * rows * width, transcendentals=rows * width),
    )(u)


def hidden_kernel(chunk, pos, near_pair, wide_pair, weight, keep, send, mine, lhs):
    x, y, z, c = pos[0], pos[1], pos[2], pos[3]

    @pl.when(pl.program_id(0) == 0)
    def _():
        for c_rel in range(2):
            core = jnp.bitwise_xor(c, c_rel)
            for j, flip in enumerate(ring_order(chunk, core)):
                source = 2 * jnp.bitwise_xor(y, flip) + core
                for x_rel, x_flip in enumerate(ring_order(chunk, c)):
                    ref = near_pair if x_rel < 2 else wide_pair
                    lhs[4 * c_rel + j, jnp.bitwise_xor(x, x_flip)] = ref[x_rel % 2, source]
        source = 2 * z + x // 2
        for x_rel, x_flip in enumerate(ring_order(chunk, c)):
            ref = near_pair if x_rel < 2 else wide_pair
            rows = ref[x_rel % 2, source].astype(F32)
            picked = jnp.where(lax.rem(x, 2) == 0, rows[:8], rows[8:])
            mine[jnp.bitwise_xor(x, x_flip)] = picked

    part = 256

    @pl.loop(0, weight.shape[0] // part)
    def _(index):
        columns = pl.ds(pl.multiple_of(index * part, part), part)
        product = nt_dot(lhs[...].reshape(512, -1), weight[columns, :]).astype(BF)
        keep[:, :, columns] = product[:256].reshape(4, 64, part)
        send[:, :, columns] = product[256:].reshape(4, 64, part)


def hidden_product(chunk, pos, near_pair, wide_pair, weight):
    width, depth = weight.shape
    tile = min(512, width)
    out_block = pl.BlockSpec((4, 64, tile), lambda i: (0, 0, i))
    return pl.pallas_call(
        functools.partial(hidden_kernel, chunk),
        grid=(width // tile,),
        in_specs=[
            SMEM,
            full(near_pair.shape),
            full(wide_pair.shape),
            pl.BlockSpec((tile, depth), lambda i: (i, 0)),
        ],
        out_specs=[out_block, out_block, full((4, 8, depth))],
        out_shape=[
            jax.ShapeDtypeStruct((4, 64, width), BF),
            jax.ShapeDtypeStruct((4, 64, width), BF),
            jax.ShapeDtypeStruct((4, 8, depth), F32),
        ],
        scratch_shapes=[pltpu.VMEM((8, 4, 16, depth), BF)],
        compiler_params=pltpu.CompilerParams(vmem_limit_bytes=16 * 2**20),
        cost_estimate=pl.CostEstimate(
            flops=2 * 512 * width * depth, bytes_accessed=2 * (width * depth + 512 * (width + depth)), transcendentals=0
        ),
    )(pos, near_pair, wide_pair, weight)


def feature_kernel(chunk, pos, near_same, wide_same, other, weight, keep, send, lhs, result):
    x, y, z, c = pos[0], pos[1], pos[2], pos[3]

    @pl.when(pl.program_id(0) == 0)
    def _():
        for j, flip in enumerate(ring_order(chunk, c)):
            lhs[2 * jnp.bitwise_xor(y, flip) + c] = (near_same if j < 2 else wide_same)[j % 2]
        for j, flip in enumerate(ring_order(chunk, 1 - c)):
            lhs[2 * jnp.bitwise_xor(y, flip) + 1 - c] = other[j]


    @pl.loop(0, 2)
    def _(index):
        part = pl.ds(4 * index, 4)
        result[part] = nt_dot(lhs[part].reshape(256, -1), weight[...]).reshape(4, *result.shape[1:])

    for x_rel, x_flip in enumerate(ring_order(chunk, c)):
        to = jnp.bitwise_xor(x, x_flip)
        out = keep if x_rel < 2 else send
        for z_rel, z_flip in enumerate((0, 2, 1, 3)):
            rows = result[2 * jnp.bitwise_xor(z, z_flip) + to // 2, :, lax.rem(to, 2)]
            out[x_rel % 2, z_rel] = rows.reshape(32, -1).astype(BF)


def feature_product(chunk, pos, pairs, weight):
    width, depth = weight.shape
    tile = min(256, width)
    out_block = pl.BlockSpec((2, 4, 32, tile), lambda i: (0, 0, 0, i))
    return pl.pallas_call(
        functools.partial(feature_kernel, chunk),
        grid=(width // tile,),
        in_specs=[SMEM] + [full(pair.shape) for pair in pairs] + [pl.BlockSpec((tile, depth), lambda i: (i, 0))],
        out_specs=[out_block, out_block],
        out_shape=[jax.ShapeDtypeStruct((2, 4, 32, width), BF)] * 2,
        scratch_shapes=[pltpu.VMEM((8, 64, depth), BF), pltpu.VMEM((8, 4, 2, 8, tile), F32)],
        compiler_params=pltpu.CompilerParams(vmem_limit_bytes=20 * 2**20),
        cost_estimate=pl.CostEstimate(
            flops=2 * 512 * width * depth, bytes_accessed=2 * (width * depth + 512 * (width + depth)), transcendentals=0
        ),
    )(pos, *pairs, weight)


def add(*terms):
    return functools.reduce(jnp.add, [term.astype(F32) for term in terms])


def sort_flips(pieces, at):
    a0, a1, a2, a3 = pieces
    odd, high = at % 2 == 1, at >= 2
    a0, a1 = jnp.where(odd, a1, a0), jnp.where(odd, a0, a1)
    a2, a3 = jnp.where(odd, a3, a2), jnp.where(odd, a2, a3)
    a0, a2 = jnp.where(high, a2, a0), jnp.where(high, a0, a2)
    a1, a3 = jnp.where(high, a3, a1), jnp.where(high, a1, a3)
    return a0, a1, a2, a3


def own_features(rows, y, c):
    depth = rows.shape[1] // 8
    parts = [jnp.stack([rows[:, (2 * i + core) * depth :][:, :depth] for i in range(4)]) for core in range(2)]
    low = c == 0
    mine = jnp.where(low, parts[0], parts[1])
    other = move_core(jnp.where(low, parts[1], parts[0]))
    both = jnp.stack([jnp.where(low, mine, other), jnp.where(low, other, mine)], axis=1)

    def block(flip):
        return lax.dynamic_index_in_dim(both, y ^ flip, 0, keepdims=False)

    pieces = [block(0)] + [move_y(block(flip), flip) for flip in (1, 2, 3)]
    return jnp.concatenate(sort_flips(pieces, y)).transpose(1, 0, 2)


def gather_rows(chunk, a3, z):
    a1 = move_z(a3, 2)
    a2, a0 = move_z(jnp.stack([a3, a1]), 1)
    own = jnp.concatenate(sort_flips((a0, a1, a2, a3), z)).transpose(1, 0, 2)
    return gather_ring(chunk, own, "x")


def gather_ring(chunk, block, axis):
    first, second = flips(chunk)
    pair = jnp.stack([block, move_ring(block, axis, first)])
    return pair, move_ring(pair, axis, second)


def reduce_hidden(chunk, keep, send):
    second, first = flips(chunk)
    other = move_core(send)
    far = move_ring(add(keep[2:], other[2:]).astype(BF), "y", first)
    last = move_ring(add(keep[1], other[1], far[1]).astype(BF), "y", second)
    return add(keep[0], other[0], far[0], last)


def reduce_x(chunk, keep, send):
    second, first = flips(chunk)
    far = move_ring(send, "x", first)
    last = move_ring(add(keep[1], far[1]).astype(BF), "x", second)
    return add(keep[0], far[0], last)


def reduce_z(totals):
    total = jnp.stack(totals, axis=1)
    far = move_z(total[2:].astype(BF), 1)
    last = move_z(add(total[1], far[1]).astype(BF), 2)
    return list(add(total[0], far[0], last))


def sum_over_dp(array):
    array = array + move_core(array)
    array = array + move_y(array, 1)
    return array + move_y(array, 3)


def per_device(
    loss_sensitivity_outgoing,
    expansion_factor,
    contraction_factor,
    intermediate_affine_values,
    centered_unscaled_entry,
    inverse_spread_per_position,
    layernorm_multiplier,
):
    x, y, z, c = (lax.axis_index(name) for name in ("x", "y", "z", "core"))
    pos = jnp.stack([x, y, z, c]).astype(jnp.int32)
    model = 8 * expansion_factor.shape[1]
    rows = own_features(loss_sensitivity_outgoing[0], y, c)
    slope = slope_rows(intermediate_affine_values[0])

    def by_chunk(array):
        rest = array.shape[1:]
        array = array.reshape(2, 4, CHUNKS, ROWS, *rest)
        array = array.transpose(2, 1, 0, 3, *range(4, array.ndim))
        return array.reshape(CHUNKS, 32, *rest)

    entry = by_chunk(centered_unscaled_entry[0]).astype(F32)
    spread = by_chunk(inverse_spread_per_position[0])
    gain = layernorm_multiplier[0]

    rows = [move_mirror(rows[: 2 * ROWS]), move_mirror(rows[2 * ROWS :])]
    rows = [rows[0][:ROWS], rows[0][ROWS:], rows[1]]
    mine, totals = [], []
    for k in range(CHUNKS):
        gathered = gather_rows(k, rows[k], z)
        keep, send, own_rows = hidden_product(k, pos, *gathered, contraction_factor[0])
        block = (reduce_hidden(k, keep, send) * slope[k]).astype(BF)
        near_pair, wide_pair = gather_ring(k, block, "y")
        pairs = (near_pair, wide_pair, move_core(jnp.concatenate([near_pair, wide_pair])))
        keep, send = feature_product(k, pos, pairs, expansion_factor[0])
        mine.append(own_rows.reshape(32, -1))
        totals.append(reduce_x(k, keep, send))
    scaled = [gain * total for total in reduce_z(totals[:1]) + reduce_z(totals[1:])]
    scaled = jnp.stack(scaled)
    upstream = jnp.stack(mine)
    sums = sum_over_dp(jnp.stack([jnp.sum(scaled, axis=2), jnp.sum(scaled * entry, axis=2)]))
    result = upstream + spread[:, :, None] * (
        scaled - sums[0][:, :, None] / model - entry * sums[1][:, :, None] / model
    )
    result = result.reshape(CHUNKS, 4, 2, ROWS, -1).transpose(2, 1, 0, 3, 4)
    return result.reshape(1, 96, -1).astype(BF)


def solution(mesh):
    split = Mesh(mesh.devices.reshape(2, 4, 2, 4, 4), ("section", "y", "core", "z", "x"))
    dp, mp = ("y", "core"), ("z", "x")
    in_specs = (
        P("section", dp + mp, None),
        P("section", dp, mp),
        P("section", mp, dp),
        P("section", dp, mp),
        P("section", mp, dp),
        P("section", mp),
        P("section", dp),
    )
    out_specs = P("section", mp, dp)
    return jax.shard_map(per_device, mesh=split, in_specs=in_specs, out_specs=out_specs, check_vma=False)
```

```python
import functools
import math

import jax
import jax.numpy as jnp
from jax import lax
from jax.experimental import pallas as pl
from jax.experimental.pallas import tpu as pltpu
from jax.sharding import Mesh, PartitionSpec as P

BF = jnp.bfloat16
F32 = jnp.float32
CHUNKS = 3
ROWS = 12 // CHUNKS


def near(core):
    return 1 + 2 * core


def wide(core):
    return 3 - 2 * core


def move_ring(array, axis, flip):
    pairs = [(c, i, c, i ^ flip(c)) for c in range(2) for i in range(4)]
    if axis == "y":
        return lax.ppermute(array, ("y", "core"), [(2 * i + c, 2 * j + d) for c, i, d, j in pairs])
    return lax.ppermute(array, ("core", axis), [(4 * c + i, 4 * d + j) for c, i, d, j in pairs])


def move_y(array, flip):
    return lax.ppermute(array, "y", [(y, y ^ flip) for y in range(4)])


def move_z(array, flip):
    return lax.ppermute(array, "z", [(z, z ^ flip) for z in range(4)])


def move_mirror(array):
    return lax.ppermute(array, ("section", "z"), [(i, 7 - i) for i in range(8)])


def move_core(array):
    return lax.ppermute(array, "core", [(0, 1), (1, 0)])


def flips(chunk):
    return (near, wide) if chunk % 2 == 0 else (wide, near)


def ring_order(chunk, core):
    first, second = flips(chunk)
    return 0, first(core), second(core), 2


def ring_flip(chunk, core, index):
    _, first, second, _ = ring_order(chunk, core)
    return jnp.where(index == 0, 0, jnp.where(index == 1, first, jnp.where(index == 2, second, 2)))


def gelu_slope(u):
    c = math.sqrt(2.0 / math.pi)
    t = jnp.tanh(c * (u + 0.044715 * u * u * u))
    return 0.5 * (1.0 + t) + 0.5 * u * (1.0 - t * t) * c * (1.0 + 3.0 * 0.044715 * u * u)


def nt_dot(left, right):
    return lax.dot_general(left, right, (((1,), (1,)), ((), ())), preferred_element_type=F32)


def full(shape):
    return pl.BlockSpec(shape, lambda i: (0,) * len(shape))


SMEM = pl.BlockSpec(memory_space=pltpu.SMEM)


def slope_kernel(u, *outs):
    values = gelu_slope(u[...].astype(F32))
    for k in range(CHUNKS):
        pieces = []
        for x in range(4):
            for z in range(4):
                start = (4 * z + x) * 12 + ROWS * k
                pieces.append(values[start : start + ROWS])
        outs[k][...] = jnp.concatenate(pieces, axis=0)


def slope_rows(u):
    rows, width = u.shape
    tile = min(256, width)
    return pl.pallas_call(
        slope_kernel,
        grid=(width // tile,),
        in_specs=[pl.BlockSpec((rows, tile), lambda i: (0, i))],
        out_specs=[pl.BlockSpec((rows // CHUNKS, tile), lambda i: (0, i))] * CHUNKS,
        out_shape=[jax.ShapeDtypeStruct((rows // CHUNKS, width), F32)] * CHUNKS,
        compiler_params=pltpu.CompilerParams(vmem_limit_bytes=16 * 2**20),
        cost_estimate=pl.CostEstimate(flops=20 * rows * width, bytes_accessed=6 * rows * width, transcendentals=rows * width),
    )(u)


def hidden_kernel(chunk, pos, near_pair, wide_pair, weight, keep, send, mine, lhs):
    x, y, z, c = pos[0], pos[1], pos[2], pos[3]

    @pl.when(pl.program_id(0) == 0)
    def _():
        @pl.loop(0, 8)
        def _(to):
            core = jnp.bitwise_xor(c, to // 4)
            source = 2 * jnp.bitwise_xor(y, ring_flip(chunk, core, lax.rem(to, 4))) + core
            for x_rel, x_flip in enumerate(ring_order(chunk, c)):
                ref = near_pair if x_rel < 2 else wide_pair
                lhs[to, jnp.bitwise_xor(x, x_flip)] = ref[x_rel % 2, source]

        source = 2 * z + x // 2
        for x_rel, x_flip in enumerate(ring_order(chunk, c)):
            ref = near_pair if x_rel < 2 else wide_pair
            rows = ref[x_rel % 2, source].astype(F32)
            picked = jnp.where(lax.rem(x, 2) == 0, rows[:8], rows[8:])
            mine[jnp.bitwise_xor(x, x_flip)] = picked

    part = 256

    @pl.loop(0, weight.shape[0] // part)
    def _(index):
        columns = pl.ds(pl.multiple_of(index * part, part), part)
        product = nt_dot(lhs[...].reshape(512, -1), weight[columns, :]).astype(BF)
        keep[:, :, columns] = product[:256].reshape(4, 64, part)
        send[:, :, columns] = product[256:].reshape(4, 64, part)


def hidden_product(chunk, pos, near_pair, wide_pair, weight):
    width, depth = weight.shape
    tile = min(512, width)
    out_block = pl.BlockSpec((4, 64, tile), lambda i: (0, 0, i))
    return pl.pallas_call(
        functools.partial(hidden_kernel, chunk),
        grid=(width // tile,),
        in_specs=[
            SMEM,
            full(near_pair.shape),
            full(wide_pair.shape),
            pl.BlockSpec((tile, depth), lambda i: (i, 0)),
        ],
        out_specs=[out_block, out_block, full((4, 8, depth))],
        out_shape=[
            jax.ShapeDtypeStruct((4, 64, width), BF),
            jax.ShapeDtypeStruct((4, 64, width), BF),
            jax.ShapeDtypeStruct((4, 8, depth), F32),
        ],
        scratch_shapes=[pltpu.VMEM((8, 4, 16, depth), BF)],
        compiler_params=pltpu.CompilerParams(vmem_limit_bytes=13 * 2**20),
        cost_estimate=pl.CostEstimate(
            flops=2 * 512 * width * depth, bytes_accessed=2 * (width * depth + 512 * (width + depth)), transcendentals=0
        ),
    )(pos, near_pair, wide_pair, weight)


def feature_kernel(chunk, pos, same, other, weight, keep, send, lhs, result):
    x, y, z, c = pos[0], pos[1], pos[2], pos[3]

    @pl.when(pl.program_id(0) == 0)
    def _():
        @pl.loop(0, 4)
        def _(j):
            lhs[2 * jnp.bitwise_xor(y, ring_flip(chunk, c, j)) + c] = same[j]
            lhs[2 * jnp.bitwise_xor(y, ring_flip(chunk, 1 - c, j)) + 1 - c] = other[j]


    @pl.loop(0, 2)
    def _(index):
        part = pl.ds(4 * index, 4)
        result[part] = nt_dot(lhs[part].reshape(256, -1), weight[...]).reshape(4, *result.shape[1:])

    for x_rel, x_flip in enumerate(ring_order(chunk, c)):
        to = jnp.bitwise_xor(x, x_flip)
        out = keep if x_rel < 2 else send
        for z_rel, z_flip in enumerate((0, 2, 1, 3)):
            rows = result[2 * jnp.bitwise_xor(z, z_flip) + to // 2, :, lax.rem(to, 2)]
            out[x_rel % 2, z_rel] = rows.reshape(32, -1).astype(BF)


def feature_product(chunk, pos, pairs, weight):
    width, depth = weight.shape
    tile = min(256, width)
    out_block = pl.BlockSpec((2, 4, 32, tile), lambda i: (0, 0, 0, i))
    return pl.pallas_call(
        functools.partial(feature_kernel, chunk),
        grid=(width // tile,),
        in_specs=[SMEM] + [full(pair.shape) for pair in pairs] + [pl.BlockSpec((tile, depth), lambda i: (i, 0))],
        out_specs=[out_block, out_block],
        out_shape=[jax.ShapeDtypeStruct((2, 4, 32, width), BF)] * 2,
        scratch_shapes=[pltpu.VMEM((8, 64, depth), BF), pltpu.VMEM((8, 4, 2, 8, tile), F32)],
        compiler_params=pltpu.CompilerParams(vmem_limit_bytes=14 * 2**20),
        cost_estimate=pl.CostEstimate(
            flops=2 * 512 * width * depth, bytes_accessed=2 * (width * depth + 512 * (width + depth)), transcendentals=0
        ),
    )(pos, *pairs, weight)


def add(*terms):
    return functools.reduce(jnp.add, [term.astype(F32) for term in terms])


def sort_flips(pieces, at):
    a0, a1, a2, a3 = pieces
    odd, high = at % 2 == 1, at >= 2
    a0, a1 = jnp.where(odd, a1, a0), jnp.where(odd, a0, a1)
    a2, a3 = jnp.where(odd, a3, a2), jnp.where(odd, a2, a3)
    a0, a2 = jnp.where(high, a2, a0), jnp.where(high, a0, a2)
    a1, a3 = jnp.where(high, a3, a1), jnp.where(high, a1, a3)
    return a0, a1, a2, a3


def own_features(rows, y, c):
    depth = rows.shape[1] // 8
    parts = [jnp.stack([rows[:, (2 * i + core) * depth :][:, :depth] for i in range(4)]) for core in range(2)]
    low = c == 0
    mine = jnp.where(low, parts[0], parts[1])
    other = move_core(jnp.where(low, parts[1], parts[0]))
    both = jnp.stack([jnp.where(low, mine, other), jnp.where(low, other, mine)], axis=1)

    def block(flip):
        return lax.dynamic_index_in_dim(both, y ^ flip, 0, keepdims=False)

    pieces = [block(0)] + [move_y(block(flip), flip) for flip in (1, 2, 3)]
    return jnp.concatenate(sort_flips(pieces, y)).transpose(1, 0, 2)


def gather_rows(chunk, part, z):
    a3 = move_mirror(part)
    a1 = move_z(a3, 2)
    a2, a0 = move_z(jnp.stack([a3, a1]), 1)
    own = jnp.concatenate(sort_flips((a0, a1, a2, a3), z)).transpose(1, 0, 2)
    return gather_ring(chunk, own, "x")


def gather_ring(chunk, block, axis):
    first, second = flips(chunk)
    pair = jnp.stack([block, move_ring(block, axis, first)])
    return pair, move_ring(pair, axis, second)


def reduce_hidden(chunk, keep, send):
    second, first = flips(chunk)
    other = move_core(send)
    far = move_ring(add(keep[2:], other[2:]).astype(BF), "y", first)
    last = move_ring(add(keep[1], other[1], far[1]).astype(BF), "y", second)
    return add(keep[0], other[0], far[0], last)


def reduce_x(chunk, keep, send):
    second, first = flips(chunk)
    far = move_ring(send, "x", first)
    last = move_ring(add(keep[1], far[1]).astype(BF), "x", second)
    return add(keep[0], far[0], last)


def reduce_z(totals):
    total = jnp.stack(totals, axis=1)
    far = move_z(total[2:].astype(BF), 1)
    last = move_z(add(total[1], far[1]).astype(BF), 2)
    return list(add(total[0], far[0], last))


def sum_over_dp(array):
    array = array + move_core(array)
    array = array + move_y(array, 1)
    return array + move_y(array, 3)


def per_device(
    loss_sensitivity_outgoing,
    expansion_factor,
    contraction_factor,
    intermediate_affine_values,
    centered_unscaled_entry,
    inverse_spread_per_position,
    layernorm_multiplier,
):
    x, y, z, c = (lax.axis_index(name) for name in ("x", "y", "z", "core"))
    pos = jnp.stack([x, y, z, c]).astype(jnp.int32)
    model = 8 * expansion_factor.shape[1]
    rows = own_features(loss_sensitivity_outgoing[0], y, c)
    slope = slope_rows(intermediate_affine_values[0])

    def by_chunk(array):
        rest = array.shape[1:]
        array = array.reshape(2, 4, CHUNKS, ROWS, *rest)
        array = array.transpose(2, 1, 0, 3, *range(4, array.ndim))
        return array.reshape(CHUNKS, 32, *rest)

    entry = by_chunk(centered_unscaled_entry[0]).astype(F32)
    spread = by_chunk(inverse_spread_per_position[0])
    gain = layernorm_multiplier[0]

    mine, totals = [], []
    for k in range(CHUNKS):
        gathered = gather_rows(k, rows[ROWS * k : ROWS * (k + 1)], z)
        keep, send, own_rows = hidden_product(k, pos, *gathered, contraction_factor[0])
        block = (reduce_hidden(k, keep, send) * slope[k]).astype(BF)
        near_pair, wide_pair = gather_ring(k, block, "y")
        same = jnp.concatenate([near_pair, wide_pair])
        pairs = (same, move_core(same))
        keep, send = feature_product(k, pos, pairs, expansion_factor[0])
        mine.append(own_rows.reshape(32, -1))
        totals.append(reduce_x(k, keep, send))
    scaled = [gain * total for total in reduce_z(totals[:1]) + reduce_z(totals[1:])]
    scaled = jnp.stack(scaled)
    upstream = jnp.stack(mine)
    sums = sum_over_dp(jnp.stack([jnp.sum(scaled, axis=2), jnp.sum(scaled * entry, axis=2)]))
    result = upstream + spread[:, :, None] * (
        scaled - sums[0][:, :, None] / model - entry * sums[1][:, :, None] / model
    )
    result = result.reshape(CHUNKS, 4, 2, ROWS, -1).transpose(2, 1, 0, 3, 4)
    return result.reshape(1, 96, -1).astype(BF)


def solution(mesh):
    split = Mesh(mesh.devices.reshape(2, 4, 2, 4, 4), ("section", "y", "core", "z", "x"))
    dp, mp = ("y", "core"), ("z", "x")
    in_specs = (
        P("section", dp + mp, None),
        P("section", dp, mp),
        P("section", mp, dp),
        P("section", dp, mp),
        P("section", mp, dp),
        P("section", mp),
        P("section", dp),
    )
    out_specs = P("section", mp, dp)
    return jax.shard_map(per_device, mesh=split, in_specs=in_specs, out_specs=out_specs, check_vma=False)
```

```python
import functools
import math

import jax
import jax.numpy as jnp
from jax import lax
from jax.experimental import pallas as pl
from jax.experimental.pallas import tpu as pltpu
from jax.sharding import Mesh, PartitionSpec as P

BF = jnp.bfloat16
F32 = jnp.float32
CHUNKS = 3
ROWS = 12 // CHUNKS


def near(core):
    return 1 + 2 * core


def wide(core):
    return 3 - 2 * core


def move_ring(array, axis, flip):
    pairs = [(c, i, c, i ^ flip(c)) for c in range(2) for i in range(4)]
    if axis == "y":
        return lax.ppermute(array, ("y", "core"), [(2 * i + c, 2 * j + d) for c, i, d, j in pairs])
    return lax.ppermute(array, ("core", axis), [(4 * c + i, 4 * d + j) for c, i, d, j in pairs])


def move_y(array, flip):
    return lax.ppermute(array, "y", [(y, y ^ flip) for y in range(4)])


def move_z(array, flip):
    return lax.ppermute(array, "z", [(z, z ^ flip) for z in range(4)])


def move_mirror(array):
    return lax.ppermute(array, ("section", "z"), [(i, 7 - i) for i in range(8)])


def move_core(array):
    return lax.ppermute(array, "core", [(0, 1), (1, 0)])


def flips(chunk):
    return (near, wide) if chunk % 2 == 0 else (wide, near)


def ring_order(chunk, core):
    first, second = flips(chunk)
    return 0, first(core), second(core), 2


def ring_flip(chunk, core, index):
    _, first, second, _ = ring_order(chunk, core)
    return jnp.where(index == 0, 0, jnp.where(index == 1, first, jnp.where(index == 2, second, 2)))


def gelu_slope(u):
    c = math.sqrt(2.0 / math.pi)
    t = jnp.tanh(c * (u + 0.044715 * u * u * u))
    return 0.5 * (1.0 + t) + 0.5 * u * (1.0 - t * t) * c * (1.0 + 3.0 * 0.044715 * u * u)


def nt_dot(left, right):
    return lax.dot_general(left, right, (((1,), (1,)), ((), ())), preferred_element_type=F32)


def full(shape):
    return pl.BlockSpec(shape, lambda i: (0,) * len(shape))


SMEM = pl.BlockSpec(memory_space=pltpu.SMEM)


def slope_kernel(u, *outs):
    values = gelu_slope(u[...].astype(F32))
    for k in range(CHUNKS):
        pieces = []
        for x in range(4):
            for z in range(4):
                start = (4 * z + x) * 12 + ROWS * k
                pieces.append(values[start : start + ROWS])
        outs[k][...] = jnp.concatenate(pieces, axis=0)


def slope_rows(u):
    rows, width = u.shape
    tile = min(256, width)
    return pl.pallas_call(
        slope_kernel,
        grid=(width // tile,),
        in_specs=[pl.BlockSpec((rows, tile), lambda i: (0, i))],
        out_specs=[pl.BlockSpec((rows // CHUNKS, tile), lambda i: (0, i))] * CHUNKS,
        out_shape=[jax.ShapeDtypeStruct((rows // CHUNKS, width), F32)] * CHUNKS,
        compiler_params=pltpu.CompilerParams(vmem_limit_bytes=16 * 2**20),
        cost_estimate=pl.CostEstimate(flops=20 * rows * width, bytes_accessed=6 * rows * width, transcendentals=rows * width),
    )(u)


def hidden_kernel(chunk, pos, near_pair, wide_pair, weight, keep, send, mine, lhs):
    x, y, z, c = pos[0], pos[1], pos[2], pos[3]

    @pl.when(pl.program_id(0) == 0)
    def _():
        @pl.loop(0, 8)
        def _(to):
            core = jnp.bitwise_xor(c, to // 4)
            source = 2 * jnp.bitwise_xor(y, ring_flip(chunk, core, lax.rem(to, 4))) + core
            for x_rel, x_flip in enumerate(ring_order(chunk, c)):
                ref = near_pair if x_rel < 2 else wide_pair
                lhs[to, jnp.bitwise_xor(x, x_flip)] = ref[x_rel % 2, source]

        source = 2 * z + x // 2
        for x_rel, x_flip in enumerate(ring_order(chunk, c)):
            ref = near_pair if x_rel < 2 else wide_pair
            rows = ref[x_rel % 2, source].astype(F32)
            picked = jnp.where(lax.rem(x, 2) == 0, rows[:8], rows[8:])
            mine[jnp.bitwise_xor(x, x_flip)] = picked

    part = 256

    @pl.loop(0, weight.shape[0] // part)
    def _(index):
        columns = pl.ds(pl.multiple_of(index * part, part), part)
        product = nt_dot(lhs[...].reshape(512, -1), weight[columns, :]).astype(BF)
        keep[:, :, columns] = product[:256].reshape(4, 64, part)
        send[:, :, columns] = product[256:].reshape(4, 64, part)


def hidden_product(chunk, pos, near_pair, wide_pair, weight):
    width, depth = weight.shape
    tile = min(512, width)
    out_block = pl.BlockSpec((4, 64, tile), lambda i: (0, 0, i))
    return pl.pallas_call(
        functools.partial(hidden_kernel, chunk),
        grid=(width // tile,),
        in_specs=[
            SMEM,
            full(near_pair.shape),
            full(wide_pair.shape),
            pl.BlockSpec((tile, depth), lambda i: (i, 0)),
        ],
        out_specs=[out_block, out_block, full((4, 8, depth))],
        out_shape=[
            jax.ShapeDtypeStruct((4, 64, width), BF),
            jax.ShapeDtypeStruct((4, 64, width), BF),
            jax.ShapeDtypeStruct((4, 8, depth), F32),
        ],
        scratch_shapes=[pltpu.VMEM((8, 4, 16, depth), BF)],
        compiler_params=pltpu.CompilerParams(vmem_limit_bytes=13 * 2**20),
        cost_estimate=pl.CostEstimate(
            flops=2 * 512 * width * depth, bytes_accessed=2 * (width * depth + 512 * (width + depth)), transcendentals=0
        ),
    )(pos, near_pair, wide_pair, weight)


def feature_kernel(chunk, pos, same, other, weight, keep, send, lhs, result):
    x, y, z, c = pos[0], pos[1], pos[2], pos[3]

    @pl.when(pl.program_id(0) == 0)
    def _():
        @pl.loop(0, 4)
        def _(j):
            lhs[2 * jnp.bitwise_xor(y, ring_flip(chunk, c, j)) + c] = same[j]
            lhs[2 * jnp.bitwise_xor(y, ring_flip(chunk, 1 - c, j)) + 1 - c] = other[j]


    rows = lhs[...].reshape(512, -1)
    result[...] = nt_dot(rows, weight[...]).reshape(result.shape)
    for x_rel, x_flip in enumerate(ring_order(chunk, c)):
        to = jnp.bitwise_xor(x, x_flip)
        out = keep if x_rel < 2 else send
        for z_rel, z_flip in enumerate((0, 2, 1, 3)):
            rows = result[2 * jnp.bitwise_xor(z, z_flip) + to // 2, :, lax.rem(to, 2)]
            out[x_rel % 2, z_rel] = rows.reshape(32, -1).astype(BF)


def feature_product(chunk, pos, pairs, weight):
    width, depth = weight.shape
    tile = min(256, width)
    out_block = pl.BlockSpec((2, 4, 32, tile), lambda i: (0, 0, 0, i))
    return pl.pallas_call(
        functools.partial(feature_kernel, chunk),
        grid=(width // tile,),
        in_specs=[SMEM] + [full(pair.shape) for pair in pairs] + [pl.BlockSpec((tile, depth), lambda i: (i, 0))],
        out_specs=[out_block, out_block],
        out_shape=[jax.ShapeDtypeStruct((2, 4, 32, width), BF)] * 2,
        scratch_shapes=[pltpu.VMEM((8, 64, depth), BF), pltpu.VMEM((8, 4, 2, 8, tile), F32)],
        compiler_params=pltpu.CompilerParams(vmem_limit_bytes=14 * 2**20),
        cost_estimate=pl.CostEstimate(
            flops=2 * 512 * width * depth, bytes_accessed=2 * (width * depth + 512 * (width + depth)), transcendentals=0
        ),
    )(pos, *pairs, weight)


def add(*terms):
    return functools.reduce(jnp.add, [term.astype(F32) for term in terms])


def sort_flips(pieces, at):
    a0, a1, a2, a3 = pieces
    odd, high = at % 2 == 1, at >= 2
    a0, a1 = jnp.where(odd, a1, a0), jnp.where(odd, a0, a1)
    a2, a3 = jnp.where(odd, a3, a2), jnp.where(odd, a2, a3)
    a0, a2 = jnp.where(high, a2, a0), jnp.where(high, a0, a2)
    a1, a3 = jnp.where(high, a3, a1), jnp.where(high, a1, a3)
    return a0, a1, a2, a3


def own_features(rows, y, c):
    depth = rows.shape[1] // 8
    parts = [jnp.stack([rows[:, (2 * i + core) * depth :][:, :depth] for i in range(4)]) for core in range(2)]
    low = c == 0
    mine = jnp.where(low, parts[0], parts[1])
    other = move_core(jnp.where(low, parts[1], parts[0]))
    both = jnp.stack([jnp.where(low, mine, other), jnp.where(low, other, mine)], axis=1)

    def block(flip):
        return lax.dynamic_index_in_dim(both, y ^ flip, 0, keepdims=False)

    pieces = [block(0)] + [move_y(block(flip), flip) for flip in (1, 2, 3)]
    return jnp.concatenate(sort_flips(pieces, y)).transpose(1, 0, 2)


def gather_z(rows, z):
    a3 = move_mirror(rows)
    a1 = move_z(a3, 2)
    a2, a0 = move_z(jnp.stack([a3, a1]), 1)
    pieces = sort_flips((a0, a1, a2, a3), z)
    starts = range(0, rows.shape[0], ROWS)
    return [jnp.concatenate([piece[at : at + ROWS] for piece in pieces]).transpose(1, 0, 2) for at in starts]


def gather_ring(chunk, block, axis):
    first, second = flips(chunk)
    pair = jnp.stack([block, move_ring(block, axis, first)])
    return pair, move_ring(pair, axis, second)


def reduce_hidden(chunk, keep, other):
    second, first = flips(chunk)
    far = move_ring(add(keep[2:], other[2:]).astype(BF), "y", first)
    last = move_ring(add(keep[1], other[1], far[1]).astype(BF), "y", second)
    return add(keep[0], other[0], far[0], last)


def reduce_features(chunk, keep, send):
    second, first = flips(chunk)
    far = move_ring(send, "x", first)
    last = move_ring(add(keep[1], far[1]).astype(BF), "x", second)
    total = add(keep[0], far[0], last)
    far = move_z(total[2:].astype(BF), 1)
    last = move_z(add(total[1], far[1]).astype(BF), 2)
    return add(total[0], far[0], last)


def sum_over_dp(array):
    array = array + move_core(array)
    array = array + move_y(array, 1)
    return array + move_y(array, 3)


def per_device(
    loss_sensitivity_outgoing,
    expansion_factor,
    contraction_factor,
    intermediate_affine_values,
    centered_unscaled_entry,
    inverse_spread_per_position,
    layernorm_multiplier,
):
    x, y, z, c = (lax.axis_index(name) for name in ("x", "y", "z", "core"))
    pos = jnp.stack([x, y, z, c]).astype(jnp.int32)
    model = 8 * expansion_factor.shape[1]
    rows = own_features(loss_sensitivity_outgoing[0], y, c)
    slope = slope_rows(intermediate_affine_values[0])

    def by_chunk(array):
        rest = array.shape[1:]
        array = array.reshape(2, 4, CHUNKS, ROWS, *rest)
        array = array.transpose(2, 1, 0, 3, *range(4, array.ndim))
        return array.reshape(CHUNKS, 32, *rest)

    entry = by_chunk(centered_unscaled_entry[0]).astype(F32)
    spread = by_chunk(inverse_spread_per_position[0])
    gain = layernorm_multiplier[0]

    parts = gather_z(rows[: 2 * ROWS], z) + gather_z(rows[2 * ROWS :], z)
    mine, keeps, others = [], [], []
    for k in range(CHUNKS):
        keep, send, own_rows = hidden_product(k, pos, *gather_ring(k, parts[k], "x"), contraction_factor[0])
        mine.append(own_rows.reshape(32, -1))
        keeps.append(keep)
        others.append(move_core(send))
    others = lax.optimization_barrier(others)
    scaled = []
    for k in range(CHUNKS):
        block = (reduce_hidden(k, keeps[k], others[k]) * slope[k]).astype(BF)
        near_pair, wide_pair = gather_ring(k, block, "y")
        same = jnp.concatenate([near_pair, wide_pair])
        pairs = (same, move_core(same))
        keep, send = feature_product(k, pos, pairs, expansion_factor[0])
        scaled.append(gain * reduce_features(k, keep, send))
    scaled = jnp.stack(scaled)
    upstream = jnp.stack(mine)
    sums = sum_over_dp(jnp.stack([jnp.sum(scaled, axis=2), jnp.sum(scaled * entry, axis=2)]))
    result = upstream + spread[:, :, None] * (
        scaled - sums[0][:, :, None] / model - entry * sums[1][:, :, None] / model
    )
    result = result.reshape(CHUNKS, 4, 2, ROWS, -1).transpose(2, 1, 0, 3, 4)
    return result.reshape(1, 96, -1).astype(BF)


def solution(mesh):
    split = Mesh(mesh.devices.reshape(2, 4, 2, 4, 4), ("section", "y", "core", "z", "x"))
    dp, mp = ("y", "core"), ("z", "x")
    in_specs = (
        P("section", dp + mp, None),
        P("section", dp, mp),
        P("section", mp, dp),
        P("section", dp, mp),
        P("section", mp, dp),
        P("section", mp),
        P("section", dp),
    )
    out_specs = P("section", mp, dp)
    return jax.shard_map(per_device, mesh=split, in_specs=in_specs, out_specs=out_specs, check_vma=False)
```

```python
import functools
import math

import jax
import jax.numpy as jnp
from jax import lax
from jax.experimental import pallas as pl
from jax.experimental.pallas import tpu as pltpu
from jax.sharding import Mesh, PartitionSpec as P

BF = jnp.bfloat16
F32 = jnp.float32
CHUNKS = 3
ROWS = 12 // CHUNKS


def near(core):
    return 1 + 2 * core


def wide(core):
    return 3 - 2 * core


def move_ring(array, axis, flip):
    pairs = [(c, i, c, i ^ flip(c)) for c in range(2) for i in range(4)]
    if axis == "y":
        return lax.ppermute(array, ("y", "core"), [(2 * i + c, 2 * j + d) for c, i, d, j in pairs])
    return lax.ppermute(array, ("core", axis), [(4 * c + i, 4 * d + j) for c, i, d, j in pairs])


def move_y(array, flip):
    return lax.ppermute(array, "y", [(y, y ^ flip) for y in range(4)])


def move_z(array, flip):
    return lax.ppermute(array, "z", [(z, z ^ flip) for z in range(4)])


def move_mirror(array):
    return lax.ppermute(array, ("section", "z"), [(i, 7 - i) for i in range(8)])


def move_core(array):
    return lax.ppermute(array, "core", [(0, 1), (1, 0)])


def flips(chunk):
    return (near, wide) if chunk % 2 == 0 else (wide, near)


def ring_order(chunk, core):
    first, second = flips(chunk)
    return 0, first(core), second(core), 2


def ring_flip(chunk, core, index):
    _, first, second, _ = ring_order(chunk, core)
    return jnp.where(index == 0, 0, jnp.where(index == 1, first, jnp.where(index == 2, second, 2)))


def gelu_slope(u):
    c = math.sqrt(2.0 / math.pi)
    t = jnp.tanh(c * (u + 0.044715 * u * u * u))
    return 0.5 * (1.0 + t) + 0.5 * u * (1.0 - t * t) * c * (1.0 + 3.0 * 0.044715 * u * u)


def nt_dot(left, right):
    return lax.dot_general(left, right, (((1,), (1,)), ((), ())), preferred_element_type=F32)


def full(shape):
    return pl.BlockSpec(shape, lambda i: (0,) * len(shape))


SMEM = pl.BlockSpec(memory_space=pltpu.SMEM)


def slope_kernel(u, *outs):
    values = gelu_slope(u[...].astype(F32))
    for k in range(CHUNKS):
        pieces = []
        for x in range(4):
            for z in range(4):
                start = (4 * z + x) * 12 + ROWS * k
                pieces.append(values[start : start + ROWS])
        outs[k][...] = jnp.concatenate(pieces, axis=0)


def slope_rows(u):
    rows, width = u.shape
    tile = min(256, width)
    return pl.pallas_call(
        slope_kernel,
        grid=(width // tile,),
        in_specs=[pl.BlockSpec((rows, tile), lambda i: (0, i))],
        out_specs=[pl.BlockSpec((rows // CHUNKS, tile), lambda i: (0, i))] * CHUNKS,
        out_shape=[jax.ShapeDtypeStruct((rows // CHUNKS, width), F32)] * CHUNKS,
        compiler_params=pltpu.CompilerParams(vmem_limit_bytes=16 * 2**20),
        cost_estimate=pl.CostEstimate(flops=20 * rows * width, bytes_accessed=6 * rows * width, transcendentals=rows * width),
    )(u)


def hidden_kernel(chunk, pos, near_pair, wide_pair, weight, keep, send, mine, lhs):
    x, y, z, c = pos[0], pos[1], pos[2], pos[3]

    @pl.when(pl.program_id(0) == 0)
    def _():
        @pl.loop(0, 8)
        def _(to):
            core = jnp.bitwise_xor(c, to // 4)
            source = 2 * jnp.bitwise_xor(y, ring_flip(chunk, core, lax.rem(to, 4))) + core
            for x_rel, x_flip in enumerate(ring_order(chunk, c)):
                ref = near_pair if x_rel < 2 else wide_pair
                lhs[to, jnp.bitwise_xor(x, x_flip)] = ref[x_rel % 2, source]

        source = 2 * z + x // 2
        for x_rel, x_flip in enumerate(ring_order(chunk, c)):
            ref = near_pair if x_rel < 2 else wide_pair
            rows = ref[x_rel % 2, source].astype(F32)
            picked = jnp.where(lax.rem(x, 2) == 0, rows[:8], rows[8:])
            mine[jnp.bitwise_xor(x, x_flip)] = picked

    part = 256

    @pl.loop(0, weight.shape[0] // part)
    def _(index):
        columns = pl.ds(pl.multiple_of(index * part, part), part)
        product = nt_dot(lhs[...].reshape(512, -1), weight[columns, :]).astype(BF)
        keep[:, :, columns] = product[:256].reshape(4, 64, part)
        send[:, :, columns] = product[256:].reshape(4, 64, part)


def hidden_product(chunk, pos, near_pair, wide_pair, weight):
    width, depth = weight.shape
    tile = min(512, width)
    out_block = pl.BlockSpec((4, 64, tile), lambda i: (0, 0, i))
    return pl.pallas_call(
        functools.partial(hidden_kernel, chunk),
        grid=(width // tile,),
        in_specs=[
            SMEM,
            full(near_pair.shape),
            full(wide_pair.shape),
            pl.BlockSpec((tile, depth), lambda i: (i, 0)),
        ],
        out_specs=[out_block, out_block, full((4, 8, depth))],
        out_shape=[
            jax.ShapeDtypeStruct((4, 64, width), BF),
            jax.ShapeDtypeStruct((4, 64, width), BF),
            jax.ShapeDtypeStruct((4, 8, depth), F32),
        ],
        scratch_shapes=[pltpu.VMEM((8, 4, 16, depth), BF)],
        compiler_params=pltpu.CompilerParams(vmem_limit_bytes=13 * 2**20),
        cost_estimate=pl.CostEstimate(
            flops=2 * 512 * width * depth, bytes_accessed=2 * (width * depth + 512 * (width + depth)), transcendentals=0
        ),
    )(pos, near_pair, wide_pair, weight)


def feature_kernel(chunk, pos, same, other, weight, keep, send, lhs, result):
    x, y, z, c = pos[0], pos[1], pos[2], pos[3]

    @pl.when(pl.program_id(0) == 0)
    def _():
        @pl.loop(0, 4)
        def _(j):
            lhs[2 * jnp.bitwise_xor(y, ring_flip(chunk, c, j)) + c] = same[j]
            lhs[2 * jnp.bitwise_xor(y, ring_flip(chunk, 1 - c, j)) + 1 - c] = other[j]


    rows = lhs[...].reshape(512, -1)
    result[...] = nt_dot(rows, weight[...]).reshape(result.shape)
    for x_rel, x_flip in enumerate(ring_order(chunk, c)):
        to = jnp.bitwise_xor(x, x_flip)
        out = keep if x_rel < 2 else send
        for z_rel, z_flip in enumerate((0, 2, 1, 3)):
            rows = result[2 * jnp.bitwise_xor(z, z_flip) + to // 2, :, lax.rem(to, 2)]
            out[x_rel % 2, z_rel] = rows.reshape(32, -1).astype(BF)


def feature_product(chunk, pos, pairs, weight):
    width, depth = weight.shape
    tile = min(256, width)
    out_block = pl.BlockSpec((2, 4, 32, tile), lambda i: (0, 0, 0, i))
    return pl.pallas_call(
        functools.partial(feature_kernel, chunk),
        grid=(width // tile,),
        in_specs=[SMEM] + [full(pair.shape) for pair in pairs] + [pl.BlockSpec((tile, depth), lambda i: (i, 0))],
        out_specs=[out_block, out_block],
        out_shape=[jax.ShapeDtypeStruct((2, 4, 32, width), BF)] * 2,
        scratch_shapes=[pltpu.VMEM((8, 64, depth), BF), pltpu.VMEM((8, 4, 2, 8, tile), F32)],
        compiler_params=pltpu.CompilerParams(vmem_limit_bytes=14 * 2**20),
        cost_estimate=pl.CostEstimate(
            flops=2 * 512 * width * depth, bytes_accessed=2 * (width * depth + 512 * (width + depth)), transcendentals=0
        ),
    )(pos, *pairs, weight)


def add(*terms):
    return functools.reduce(jnp.add, [term.astype(F32) for term in terms])


def sort_flips(pieces, at):
    a0, a1, a2, a3 = pieces
    odd, high = at % 2 == 1, at >= 2
    a0, a1 = jnp.where(odd, a1, a0), jnp.where(odd, a0, a1)
    a2, a3 = jnp.where(odd, a3, a2), jnp.where(odd, a2, a3)
    a0, a2 = jnp.where(high, a2, a0), jnp.where(high, a0, a2)
    a1, a3 = jnp.where(high, a3, a1), jnp.where(high, a1, a3)
    return a0, a1, a2, a3


def own_features(rows, y, c):
    depth = rows.shape[1] // 8
    parts = [jnp.stack([rows[:, (2 * i + core) * depth :][:, :depth] for i in range(4)]) for core in range(2)]
    low = c == 0
    mine = jnp.where(low, parts[0], parts[1])
    other = move_core(jnp.where(low, parts[1], parts[0]))
    both = jnp.stack([jnp.where(low, mine, other), jnp.where(low, other, mine)], axis=1)

    def block(flip):
        return lax.dynamic_index_in_dim(both, y ^ flip, 0, keepdims=False)

    pieces = [block(0)] + [move_y(block(flip), flip) for flip in (1, 2, 3)]
    return jnp.concatenate(sort_flips(pieces, y)).transpose(1, 0, 2)


def gather_z(rows, z):
    a3 = move_mirror(rows)
    a1 = move_z(a3, 2)
    a2, a0 = move_z(jnp.stack([a3, a1]), 1)
    pieces = sort_flips((a0, a1, a2, a3), z)
    starts = range(0, rows.shape[0], ROWS)
    return [jnp.concatenate([piece[at : at + ROWS] for piece in pieces]).transpose(1, 0, 2) for at in starts]


def gather_ring(chunk, block, axis):
    first, second = flips(chunk)
    pair = jnp.stack([block, move_ring(block, axis, first)])
    return pair, move_ring(pair, axis, second)


def reduce_hidden(chunk, keep, other):
    second, first = flips(chunk)
    far = move_ring(add(keep[2:], other[2:]).astype(BF), "y", first)
    last = move_ring(add(keep[1], other[1], far[1]).astype(BF), "y", second)
    return add(keep[0], other[0], far[0], last)


def reduce_features(chunk, keep, send):
    second, first = flips(chunk)
    far = move_ring(send, "x", first)
    last = move_ring(add(keep[1], far[1]).astype(BF), "x", second)
    total = add(keep[0], far[0], last)
    far = move_z(total[2:].astype(BF), 1)
    last = move_z(add(total[1], far[1]).astype(BF), 2)
    return add(total[0], far[0], last)


def sum_over_dp(array):
    array = array + move_core(array)
    array = array + move_y(array, 1)
    return array + move_y(array, 3)


def per_device(
    loss_sensitivity_outgoing,
    expansion_factor,
    contraction_factor,
    intermediate_affine_values,
    centered_unscaled_entry,
    inverse_spread_per_position,
    layernorm_multiplier,
):
    x, y, z, c = (lax.axis_index(name) for name in ("x", "y", "z", "core"))
    pos = jnp.stack([x, y, z, c]).astype(jnp.int32)
    model = 8 * expansion_factor.shape[1]
    rows = own_features(loss_sensitivity_outgoing[0], y, c)
    slope = slope_rows(intermediate_affine_values[0])

    def by_chunk(array):
        rest = array.shape[1:]
        array = array.reshape(2, 4, CHUNKS, ROWS, *rest)
        array = array.transpose(2, 1, 0, 3, *range(4, array.ndim))
        return array.reshape(CHUNKS, 32, *rest)

    entry = by_chunk(centered_unscaled_entry[0]).astype(F32)
    spread = by_chunk(inverse_spread_per_position[0])
    gain = layernorm_multiplier[0]

    parts = gather_z(rows[: 2 * ROWS], z) + gather_z(rows[2 * ROWS :], z)
    moved = lax.optimization_barrier([move_ring(parts[k], "x", flips(k)[0]) for k in range(CHUNKS)])
    mine, keeps, others = [], [], []
    for k in range(CHUNKS):
        near_pair = jnp.stack([parts[k], moved[k]])
        wide_pair = move_ring(near_pair, "x", flips(k)[1])
        keep, send, own_rows = hidden_product(k, pos, near_pair, wide_pair, contraction_factor[0])
        mine.append(own_rows.reshape(32, -1))
        keeps.append(keep)
        others.append(move_core(send))
    others = lax.optimization_barrier(others)
    scaled = []
    for k in range(CHUNKS):
        block = (reduce_hidden(k, keeps[k], others[k]) * slope[k]).astype(BF)
        near_pair, wide_pair = gather_ring(k, block, "y")
        same = jnp.concatenate([near_pair, wide_pair])
        pairs = (same, move_core(same))
        keep, send = feature_product(k, pos, pairs, expansion_factor[0])
        scaled.append(gain * reduce_features(k, keep, send))
    scaled = jnp.stack(scaled)
    upstream = jnp.stack(mine)
    sums = sum_over_dp(jnp.stack([jnp.sum(scaled, axis=2), jnp.sum(scaled * entry, axis=2)]))
    result = upstream + spread[:, :, None] * (
        scaled - sums[0][:, :, None] / model - entry * sums[1][:, :, None] / model
    )
    result = result.reshape(CHUNKS, 4, 2, ROWS, -1).transpose(2, 1, 0, 3, 4)
    return result.reshape(1, 96, -1).astype(BF)


def solution(mesh):
    split = Mesh(mesh.devices.reshape(2, 4, 2, 4, 4), ("section", "y", "core", "z", "x"))
    dp, mp = ("y", "core"), ("z", "x")
    in_specs = (
        P("section", dp + mp, None),
        P("section", dp, mp),
        P("section", mp, dp),
        P("section", dp, mp),
        P("section", mp, dp),
        P("section", mp),
        P("section", dp),
    )
    out_specs = P("section", mp, dp)
    return jax.shard_map(per_device, mesh=split, in_specs=in_specs, out_specs=out_specs, check_vma=False)
```
